512 devices in a mesh: seq: 64 (over z, y), tp: 8 (over x, core).
Axes of the slice: x: 4, y: 8, z: 8, core: 2. Of those that a mesh axis runs over, the one named last changes fastest.
Arguments:
- queries: bfloat16 [98304, 4096], P('seq', 'tp'), may hold values from -9 to 9
- keys: bfloat16 [98304, 1024], P('seq', 'tp'), may hold values from -10 to 10
- values: bfloat16 [98304, 1024], P('seq', 'tp'), may hold values from -12 to 12
- vertical: int32 [32, 8], replicated, may hold values from 0 to 1535, as said below
- slash: int32 [32, 2], replicated, may hold values from 0 to 8, as said below
- counts: int32 [32, 2], replicated, may hold values from 1 to 8, as said below
Outputs:
- attended: bfloat16 [98304, 4096], P(('seq', 'tp'))
The draws below stay inside these ranges and needn't reach their ends.
Inputs may be any that keep to these rules, and one draw needn't show every extreme that they name: `vertical`: each head's list holds distinct blocks and begins with block 0; slots at or past the head's count are padding. `slash`: each head's offsets are distinct and begin with 0; slots at or past the head's count are padding. Column 0 counts a head's used vertical slots (at most 8), column 1 its used slash slots (at most 2).
All inputs are finite; a program needn't handle non-finite values.
Results may differ from the reference program's by a relative error of at most 0.0033.
Values may be sent and summed in bfloat16 or wider, within the bound.
A program may use at most 64 MiB of HBM per device.

```python
import math
import jax
import jax.numpy as jnp
from jax import lax

H = 32
KVH = 8
HD = 128
BLK = 64
NV = 8
NS = 2
SREACH = 8
TOK = 98304
NB = 1536


def draw_queries(key, part):
    noise_key = jax.random.fold_in(key, 11)
    base = jnp.clip(jax.random.normal(noise_key, (TOK, H * HD), jnp.float32), -5.0, 5.0)
    return base.astype(jnp.bfloat16)


def draw_keys(key, part):
    noise_key = jax.random.fold_in(key, 17)
    base = jnp.clip(2.0 * jax.random.normal(noise_key, (TOK, KVH * HD), jnp.float32), -10.0, 10.0)
    return base.astype(jnp.bfloat16)


def head_picks(head_keys, span, taken):

    def one_head(head_key):
        return jax.random.permutation(head_key, span)[:taken]
    return jax.vmap(one_head)(head_keys)


def draw_vertical(key, part):
    head_keys = jax.random.split(jax.random.fold_in(key, 21), H)
    picks = head_picks(head_keys, NB - 2, NV - 1).astype(jnp.int32) + 1
    chosen = jax.random.randint(jax.random.fold_in(key, 22), (), 0, H)
    last_col = jnp.where(jnp.arange(H, dtype=jnp.int32) == chosen, NB - 1, picks[:, NV - 2])
    picks = picks.at[:, NV - 2].set(last_col.astype(jnp.int32))
    return jnp.concatenate([jnp.zeros((H, 1), jnp.int32), picks], axis=1)


def draw_slash(key, part):
    head_keys = jax.random.split(jax.random.fold_in(key, 25), H)
    picks = head_picks(head_keys, SREACH - 1, NS - 1).astype(jnp.int32) + 1
    chosen = jax.random.randint(jax.random.fold_in(key, 26), (), 0, H)
    last_col = jnp.where(jnp.arange(H, dtype=jnp.int32) == chosen, SREACH, picks[:, NS - 2])
    picks = picks.at[:, NS - 2].set(last_col.astype(jnp.int32))
    return jnp.concatenate([jnp.zeros((H, 1), jnp.int32), picks], axis=1)


def skewed_count(key, most):
    first = jax.random.randint(jax.random.fold_in(key, 1), (H,), 1, most + 1)
    second = jax.random.randint(jax.random.fold_in(key, 2), (H,), 1, most + 1)
    values_drawn = jnp.minimum(first, second)
    high_head = jax.random.randint(jax.random.fold_in(key, 3), (), 0, H)
    low_head = (high_head + jax.random.randint(jax.random.fold_in(key, 4), (), 1, H)) % H
    head_ids = jnp.arange(H, dtype=jnp.int32)
    values_drawn = jnp.where(head_ids == high_head, most, values_drawn)
    values_drawn = jnp.where(head_ids == low_head, 1, values_drawn)
    return values_drawn.astype(jnp.int32)


def draw_counts(key, part):
    vert_count = skewed_count(jax.random.fold_in(key, 31), NV)
    slash_count = skewed_count(jax.random.fold_in(key, 32), NS)
    return jnp.stack([vert_count, slash_count], axis=1)


def block_scale(rng, shape, cuts, smallest, largest):
    def one(axis_at, parts):
        steps = jax.random.uniform(jax.random.fold_in(jax.random.fold_in(rng, 6), axis_at), (parts,), jnp.float32, smallest / len(cuts), largest / len(cuts))
        return jnp.repeat(jnp.exp(steps), shape[axis_at] // parts).reshape((-1,) + (1,) * (len(shape) - axis_at - 1))

    gain = one(*cuts[0])
    for cut in cuts[1:]:
        gain = gain * one(*cut)
    return gain


def centred(stream_key, shape, deviation, limit, cuts=(), kind=jnp.bfloat16):
    gain = block_scale(stream_key, shape, cuts, -0.22, 0.18) if cuts else 1.0
    array = jax.random.normal(stream_key, shape, jnp.float32) * deviation * gain
    return jnp.minimum(jnp.maximum(array, -limit), limit).astype(kind)


def setup_inputs(seed: int = 0) -> dict:
    seeds = jax.random.split(jax.random.key(seed), 7)
    return {
        "queries": draw_queries(jax.random.fold_in(seeds[6], 71), 0),
        "keys": draw_keys(jax.random.fold_in(seeds[6], 71), 0),
        "values": centred(seeds[2], (TOK, KVH * HD), 2.0, 12.0, ((0, 64), (1, 8))),
        "vertical": draw_vertical(jax.random.fold_in(seeds[6], 71), 0),
        "slash": draw_slash(jax.random.fold_in(seeds[6], 71), 0),
        "counts": draw_counts(jax.random.fold_in(seeds[6], 71), 0),
    }


NEG_BIG = -1e+30

def reference(queries, keys, values, vertical, slash, counts):
    group_size = H // KVH
    score_scale_factor = 1.0 / math.sqrt(HD)
    key_offset = jnp.arange(BLK, dtype=jnp.int32)
    block_ids = jnp.arange(NB, dtype=jnp.int32)
    query_pos = block_ids[:, None] * BLK + key_offset[None, :]
    query_all = queries.reshape(TOK, H, HD)
    key_all = keys.reshape(TOK, KVH, HD)
    value_all = values.reshape(TOK, KVH, HD)

    def per_head(head_id):
        pair_id = head_id // group_size
        query_head_index = lax.dynamic_index_in_dim(query_all, head_id, 1, False).astype(jnp.float32).reshape(NB, BLK, HD)
        key_head = lax.dynamic_index_in_dim(key_all, pair_id, 1, False).reshape(NB, BLK, HD)
        value_head = lax.dynamic_index_in_dim(value_all, pair_id, 1, False).reshape(NB, BLK, HD)
        vert_list = vertical[head_id]
        slash_list = slash[head_id]
        vert_valid = jnp.arange(NV, dtype=jnp.int32) < counts[head_id, 0]
        slash_valid = jnp.arange(NS, dtype=jnp.int32) < counts[head_id, 1]
        vertical_line_keys = key_head[vert_list].astype(jnp.float32)
        vertical_line_values = value_head[vert_list].astype(jnp.float32)
        vertical_line_score = jnp.einsum('itp,ofp->itof', query_head_index, vertical_line_keys) * score_scale_factor
        vert_pos = vert_list[:, None] * BLK + key_offset[None, :]
        vert_mask = vert_valid[None, None, :, None] & (vert_pos[None, None, :, :] <= query_pos[:, :, None, None])
        global_block = block_ids[:, None] - slash_list[None, :]
        listed = jnp.any((global_block[:, :, None] == vert_list[None, None, :]) & vert_valid[None, None, :], axis=2)
        block_mask = slash_valid[None, :] & (global_block >= 0) & jnp.logical_not(listed)
        safe_block = jnp.maximum(global_block, 0)
        diagonal_keys = key_head[safe_block].astype(jnp.float32)
        diagonal_values = value_head[safe_block].astype(jnp.float32)
        slash_pos = safe_block[:, :, None] * BLK + key_offset[None, None, :]
        slash_mask = block_mask[:, None, :, None] & (slash_pos[:, None, :, :] <= query_pos[:, :, None, None])
        diagonal_score = jnp.einsum('tfx,tywx->tfyw', query_head_index, diagonal_keys) * score_scale_factor
        vertical_line_score = jnp.where(vert_mask, vertical_line_score, NEG_BIG)
        diagonal_score = jnp.where(slash_mask, diagonal_score, NEG_BIG)
        top = jnp.maximum(lax.optimization_barrier(jnp.max(vertical_line_score, axis=(2, 3))), lax.optimization_barrier(jnp.max(diagonal_score, axis=(2, 3))))
        vert_prob = jnp.where(vert_mask, jnp.exp(vertical_line_score - top[:, :, None, None]), 0.0)
        slash_prob = jnp.where(slash_mask, jnp.exp(diagonal_score - top[:, :, None, None]), 0.0)
        total = lax.optimization_barrier(jnp.sum(vert_prob, axis=(2, 3))) + lax.optimization_barrier(jnp.sum(slash_prob, axis=(2, 3)))
        vertical_line_weight = lax.optimization_barrier(vert_prob.astype(jnp.bfloat16)).astype(jnp.float32)
        diagonal_weight = lax.optimization_barrier(slash_prob.astype(jnp.bfloat16)).astype(jnp.float32)
        numerator_rows = jnp.einsum('nxmr,mrc->nxc', vertical_line_weight, vertical_line_values)
        numerator_rows = numerator_rows + jnp.einsum('mnzt,mztx->mnx', diagonal_weight, diagonal_values)
        return (numerator_rows / total[:, :, None]).astype(jnp.bfloat16).reshape(TOK, HD)
    head_outs = lax.map(per_head, jnp.arange(H, dtype=jnp.int32))
    return jnp.transpose(head_outs, (1, 0, 2)).reshape(TOK, H * HD)
```

```python
import functools
import math

import jax
import jax.numpy as jnp
from jax import lax
from jax.experimental import pallas as pl
from jax.experimental.pallas import tpu as pltpu
from jax.sharding import PartitionSpec as P

HD = 128
BLK = 64
NV = 8
NS = 2
SREACH = 8
HALO = SREACH * BLK

BIG = 1 << 30
NEG = -1e30
EXP2_SCALE = math.log2(math.e) / math.sqrt(HD)
MESH = pl.DeviceIdType.MESH


def attend_tile(row0, tile, head, slot0, refs):
    q_ref, wk, wv, gk, gv, kpos_v, kpos_s, off_ref, seq0 = refs
    q = q_ref[pl.ds(row0, tile), pl.ds(pl.multiple_of(head * HD, HD), HD)]
    rows = lax.broadcasted_iota(jnp.int32, (tile, HD), 0) + (seq0 + row0)
    kt = (((1,), (1,)), ((), ()))
    vert_k = gk[pl.ds(slot0, NV * BLK), :]
    vert_v = gv[pl.ds(slot0, NV * BLK), :]
    sv = lax.dot_general(q, vert_k, kt, preferred_element_type=jnp.float32)
    pair = 2 * BLK
    r_i = lax.broadcasted_iota(jnp.int32, (pair, HD), 0)
    c_i = lax.broadcasted_iota(jnp.int32, (pair, HD), 1)
    straight = (r_i < BLK) == (c_i < BLK)
    off0, off1 = off_ref
    vals = []
    ss = []
    for p in range(tile // pair):
        start = row0 + p * pair + HALO
        s0 = start + off0 * -BLK
        s1 = start + off1 * -BLK
        s1b = s1 + BLK
        k2 = jnp.concatenate(
            [wk[pl.ds(s0, pair), :], wk[pl.ds(s1b, BLK), :], wk[pl.ds(s1, BLK), :]], axis=0
        )
        v2 = jnp.concatenate(
            [wv[pl.ds(s0, pair), :], wv[pl.ds(s1b, BLK), :], wv[pl.ds(s1, BLK), :]], axis=0
        )
        both = lax.dot_general(
            q[p * pair : (p + 1) * pair], k2, kt, preferred_element_type=jnp.float32
        )
        score = jnp.where(straight, both[:, :pair], both[:, pair:])
        block = (row0 + p * pair) // BLK
        kp0 = jnp.broadcast_to(kpos_s[pl.ds(block, 1), :], (BLK, HD))
        kp1 = jnp.broadcast_to(kpos_s[pl.ds(block + 1, 1), :], (BLK, HD))
        kp = jnp.concatenate([kp0, kp1], axis=0)
        ss.append(jnp.where(kp <= rows[p * pair : (p + 1) * pair], score, NEG))
        vals.append(v2)
    ss = jnp.concatenate(ss, axis=0)
    parts = []
    for k in range(NV * BLK // HD):
        kp = kpos_v[0:1, k * HD : (k + 1) * HD]
        parts.append(jnp.where(kp <= rows, sv[:, k * HD : (k + 1) * HD], NEG))
    top = ss
    for part in parts:
        top = jnp.maximum(top, part)
    top = jnp.max(top, axis=1, keepdims=True)
    ps = jnp.exp2((ss - top) * EXP2_SCALE)
    total = ps
    probs = []
    for part in parts:
        prob = jnp.exp2((part - top) * EXP2_SCALE)
        total = total + prob
        probs.append(prob.astype(jnp.bfloat16))
    total = jnp.sum(total, axis=1, keepdims=True)
    acc = jnp.dot(
        jnp.concatenate(probs, axis=1), vert_v, preferred_element_type=jnp.float32
    )
    slash_acc = []
    for p in range(tile // pair):
        w = ps[p * pair : (p + 1) * pair]
        w2 = jnp.concatenate(
            [
                jnp.where(straight, w, 0.0).astype(jnp.bfloat16),
                jnp.where(straight, 0.0, w).astype(jnp.bfloat16),
            ],
            axis=1,
        )
        slash_acc.append(jnp.dot(w2, vals[p], preferred_element_type=jnp.float32))
    acc = acc + jnp.concatenate(slash_acc, axis=0)
    return (acc / total).astype(jnp.bfloat16)


def key_positions(head, seq, blocks_dev, vert, slash, counts, kpos_v, kpos_s):
    n_vert = counts[head, 0]
    n_slash = counts[head, 1]
    lane = lax.broadcasted_iota(jnp.int32, (8, HD), 1)
    for k in range(NV // 2):
        pos = jnp.where(lane < BLK, vert[head, 2 * k], vert[head, 2 * k + 1]) * BLK + lane % BLK
        used = jnp.where(lane < BLK, 2 * k, 2 * k + 1) < n_vert
        kpos_v[:, k * HD : (k + 1) * HD] = jnp.where(used, pos, BIG)
    row = lax.broadcasted_iota(jnp.int32, (blocks_dev, HD), 0)
    col = lax.broadcasted_iota(jnp.int32, (blocks_dev, HD), 1)
    first = (row % 2 == 0) == (col < BLK)
    block = seq * blocks_dev + row - jnp.where(first, slash[head, 0], slash[head, 1])
    dead = (block < 0) | (jnp.where(first, 0, 1) >= n_slash)
    for j in range(NV):
        dead = dead | ((block == vert[head, j]) & (jnp.full_like(row, j) < n_vert))
    kpos_s[...] = jnp.where(dead, BIG, block * BLK + col % BLK)


def fused(
    nz, ny, ntp, slots,
    vert, slash, counts, q_hbm, k_hbm, v_hbm, out,
    q_ref, wk, wv, hk, hv, snd, got1k, got1v, mid, got2k, got2v, gk, gv, obuf, kpos_v, kpos_s,
    local_sem, halo_send, halo_recv, send1, recv1, send2, recv2, send3, recv3, send4, recv4,
    own_sem, out_send, out_recv,
):
    tok = q_ref.shape[0]
    heads = q_ref.shape[1] // HD
    blocks_dev = tok // BLK
    seq = lax.axis_index("seq")
    tp = lax.axis_index("tp")
    z, y = seq // ny, seq % ny
    nseq = nz * ny
    axes = ((ny, nz), (nz, ny))
    mine = ((y, z), (z, y))

    def at(side, first, second):
        return (second * ny + first if side == 0 else first * ny + second, tp)

    def local(i, src, dst):
        return pltpu.make_async_copy(src, dst, local_sem.at[i])

    copies = [
        local(0, k_hbm, wk.at[HALO:]),
        local(1, v_hbm, wv.at[HALO:]),
        local(2, q_hbm, q_ref),
    ]
    for c in copies:
        c.start()

    barrier = pltpu.get_barrier_semaphore()

    @pl.loop(1, ny)
    def _(d):
        peer = z * ny + lax.rem(y + d, ny)
        pl.semaphore_signal(barrier, inc=1, device_id=(peer, tp), device_id_type=MESH)

    @pl.loop(1, nz)
    def _(d):
        peer = lax.rem(z + d, nz) * ny + y
        pl.semaphore_signal(barrier, inc=1, device_id=(peer, tp), device_id_type=MESH)

    @pl.loop(1, ntp)
    def _(d):
        pl.semaphore_signal(
            barrier, inc=1, device_id=(seq, lax.rem(tp + d, ntp)), device_id_type=MESH
        )

    after, before = lax.rem(seq + 1, nseq), lax.rem(seq + nseq - 1, nseq)
    for peer in (after, before):
        pl.semaphore_signal(barrier, inc=1, device_id=(peer, tp), device_id_type=MESH)

    copies[0].wait()
    copies[1].wait()

    @pl.loop(0, slots)
    def _(slot):
        block = vert[tp * heads + slot // NV, slot % NV]
        row = lax.rem(block, blocks_dev) * BLK + HALO
        dst = pl.ds(pl.multiple_of(slot * BLK, BLK), BLK)
        snd[0, dst, :] = wk[pl.ds(row, BLK), :]
        snd[1, dst, :] = wv[pl.ds(row, BLK), :]

    pl.semaphore_wait(barrier, ny + nz + ntp - 3 + 2)

    halo = [
        pltpu.make_async_remote_copy(
            src_ref=w.at[tok : tok + HALO],
            dst_ref=dst,
            send_sem=halo_send.at[i],
            recv_sem=halo_recv.at[i],
            device_id=(after, tp),
            device_id_type=MESH,
        )
        for i, (w, dst) in enumerate(((wk, hk), (wv, hv)))
    ]

    got1, got2, full = (got1k, got1v), (got2k, got2v), (gk, gv)

    def spread1(side, d):
        n, me = axes[side][0], mine[side][0]
        rows = slots * BLK // n
        peer = lax.rem(me + d, n)
        return pltpu.make_async_remote_copy(
            src_ref=snd.at[side, pl.ds(pl.multiple_of(peer * rows, 16), rows), :],
            dst_ref=got1[side].at[pl.ds(pl.multiple_of(me * rows, 16), rows), :],
            send_sem=send1.at[side, d],
            recv_sem=recv1.at[side, n - d],
            device_id=at(side, peer, mine[side][1]),
            device_id_type=MESH,
        )

    def spread2(side, d):
        n1 = axes[side][0]
        n, me = axes[side][1], mine[side][1]
        rows = slots * BLK // n1 // n
        peer = lax.rem(me + d, n)
        return pltpu.make_async_remote_copy(
            src_ref=mid.at[side, pl.ds(pl.multiple_of(peer * rows, 16), rows), :],
            dst_ref=got2[side].at[pl.ds(pl.multiple_of(me * rows, 16), rows), :],
            send_sem=send2.at[side, d],
            recv_sem=recv2.at[side, n - d],
            device_id=at(side, mine[side][0], peer),
            device_id_type=MESH,
        )


    def gather2(side, d):
        n1, me1 = axes[side][0], mine[side][0]
        n, me = axes[side][1], mine[side][1]
        rows1 = slots * BLK // n1
        rows = rows1 // n
        place = pl.ds(pl.multiple_of(me1 * rows1 + me * rows, 16), rows)
        return pltpu.make_async_remote_copy(
            src_ref=full[side].at[place, :],
            dst_ref=full[side].at[place, :],
            send_sem=send3.at[side, d],
            recv_sem=recv3.at[side, n - d],
            device_id=at(side, me1, lax.rem(me + d, n)),
            device_id_type=MESH,
        )

    def gather1(side, d):
        n, me = axes[side][0], mine[side][0]
        rows = slots * BLK // n
        place = pl.ds(pl.multiple_of(me * rows, 16), rows)
        return pltpu.make_async_remote_copy(
            src_ref=full[side].at[place, :],
            dst_ref=full[side].at[place, :],
            send_sem=send4.at[side, d],
            recv_sem=recv4.at[side, n - d],
            device_id=at(side, lax.rem(me + d, n), mine[side][1]),
            device_id_type=MESH,
        )

    def owner(slot):
        block = vert[tp * heads + slot // NV, slot % NV]
        device = lax.div(block, blocks_dev)
        return lax.rem(device, ny), lax.div(device, ny)

    def each(side, axis, step):
        @pl.loop(1, axes[side][axis])
        def _(d):
            step(d)

    for side in (0, 1):
        each(side, 0, lambda d, side=side: spread1(side, d).start())
    for c in halo:
        c.start()

    for side in (0, 1):
        n, me = axes[side][0], mine[side][0]
        rows = slots * BLK // n
        here = pl.ds(pl.multiple_of(me * rows, 16), rows)
        got1[side][here, :] = snd[side, here, :]
        each(side, 0, lambda d, side=side: spread1(side, d).wait_recv())

        @pl.loop(0, rows // BLK)
        def _(k, side=side, rows=rows, me=me):
            first = owner(me * (rows // BLK) + k)[side]
            src = first * rows + k * BLK
            dst = pl.ds(pl.multiple_of(k * BLK, BLK), BLK)
            mid[side, dst, :] = got1[side][pl.ds(src, BLK), :]

        each(side, 1, lambda d, side=side: spread2(side, d).start())

    for side in (0, 1):
        n1, me1 = axes[side][0], mine[side][0]
        n, me = axes[side][1], mine[side][1]
        rows1 = slots * BLK // n1
        rows = rows1 // n
        piece = min(rows, BLK)
        here = pl.ds(pl.multiple_of(me * rows, 16), rows)
        got2[side][here, :] = mid[side, here, :]
        each(side, 1, lambda d, side=side: spread2(side, d).wait_recv())
        for k in range(rows // piece):
            slot = (me1 * rows1 + me * rows + k * piece) // BLK
            second = owner(slot)[1 - side]
            src = second * rows + k * piece
            dst = pl.ds(pl.multiple_of(me1 * rows1 + me * rows + k * piece, 16), piece)
            full[side][dst, :] = got2[side][pl.ds(src, piece), :]
        each(side, 1, lambda d, side=side: gather2(side, d).start())

    for side in (0, 1):
        each(side, 1, lambda d, side=side: gather2(side, d).wait_recv())
        each(side, 0, lambda d, side=side: gather1(side, d).start())

    for c in halo:
        c.wait_recv()
    joins = [local(3, hk, wk.at[0:HALO]), local(4, hv, wv.at[0:HALO])]
    for c in joins:
        c.start()
    copies[2].wait()
    for c in joins:
        c.wait()
    for side in (0, 1):
        each(side, 0, lambda d, side=side: gather1(side, d).wait_recv())

    nx = ntp // 2
    part = tok // ntp
    tile = 2 * part
    x, core = tp // 2, lax.rem(tp, 2)
    order = (2, 1, 3, 0) if nx == 4 else tuple(range(nx - 1, -1, -1))

    def send_out(h, j, c, target):
        src = pl.multiple_of(c * part, 16)
        cols = pl.ds(pl.multiple_of((tp * heads + h) * HD, HD), HD)
        return pltpu.make_async_remote_copy(
            src_ref=obuf.at[h, j, pl.ds(src, part), :],
            dst_ref=out.at[:, cols],
            send_sem=out_send.at[h, j, c],
            recv_sem=out_recv.at[h, tp],
            device_id=(seq, target),
            device_id_type=MESH,
        )

    def keep_out(h, j):
        src = pl.multiple_of(core * part, 16)
        cols = pl.ds(pl.multiple_of((tp * heads + h) * HD, HD), HD)
        return pltpu.make_async_copy(
            obuf.at[h, j, pl.ds(src, part), :], out.at[:, cols], own_sem.at[h]
        )

    def landed(h, source):
        cols = pl.ds(pl.multiple_of((source * heads + h) * HD, HD), HD)
        return pltpu.make_async_remote_copy(
            src_ref=obuf.at[h, 0, pl.ds(0, part), :],
            dst_ref=out.at[:, cols],
            send_sem=out_send.at[h, 0, 0],
            recv_sem=out_recv.at[h, source],
            device_id=(seq, source),
            device_id_type=MESH,
        )

    @pl.loop(0, heads)
    def _(h):
        head = tp * heads + h
        key_positions(head, seq, blocks_dev, vert, slash, counts, kpos_v, kpos_s)
        refs = (
            q_ref, wk, wv, gk, gv, kpos_v, kpos_s,
            (slash[head, 0], slash[head, 1]), seq * tok,
        )
        for j, step in enumerate(order):
            chip = lax.rem(x + step, nx)
            row0 = pl.multiple_of(chip * tile, BLK)
            slot0 = pl.multiple_of(h * (NV * BLK), BLK)
            obuf[h, j] = attend_tile(row0, tile, h, slot0, refs)
            if step:
                for c in (0, 1):
                    send_out(h, j, c, chip * 2 + c).start()
            else:
                send_out(h, j, 1 - core, chip * 2 + 1 - core).start()
                keep_out(h, j).start()

    @pl.loop(0, heads)
    def _(h):
        @pl.loop(1, ntp)
        def _(d):
            landed(h, lax.rem(tp + d, ntp)).wait_recv()

        keep_out(h, nx - 1).wait()
        for j, step in enumerate(order):
            chip = lax.rem(x + step, nx)
            if step:
                for c in (0, 1):
                    send_out(h, j, c, chip * 2 + c).wait_send()
            else:
                send_out(h, j, 1 - core, chip * 2 + 1 - core).wait_send()

    for c in halo:
        c.wait_send()
    for side in (0, 1):
        each(side, 0, lambda d, side=side: spread1(side, d).wait_send())
        each(side, 1, lambda d, side=side: spread2(side, d).wait_send())
        each(side, 1, lambda d, side=side: gather2(side, d).wait_send())
        each(side, 0, lambda d, side=side: gather1(side, d).wait_send())


def per_device(nz, ny, ntp, queries, keys, values, vertical, slash, counts):
    tok, width = queries.shape
    heads = width // HD
    slots = heads * NV
    part = tok // ntp
    nx = ntp // 2
    big = max(ny, nz)
    dma = pltpu.SemaphoreType.DMA
    bf = jnp.bfloat16
    smem = pl.BlockSpec(memory_space=pltpu.SMEM)
    hbm = pl.BlockSpec(memory_space=pl.ANY)
    return pl.pallas_call(
        functools.partial(fused, nz, ny, ntp, slots),
        out_shape=jax.ShapeDtypeStruct((part, width * ntp), bf),
        in_specs=[smem, smem, smem, hbm, hbm, hbm],
        out_specs=hbm,
        scratch_shapes=[
            pltpu.VMEM((tok, width), bf),
            pltpu.VMEM((HALO + tok, HD), bf),
            pltpu.VMEM((HALO + tok, HD), bf),
            pltpu.VMEM((HALO, HD), bf),
            pltpu.VMEM((HALO, HD), bf),
            pltpu.VMEM((2, slots * BLK, HD), bf),
            pltpu.VMEM((slots * BLK, HD), bf),
            pltpu.VMEM((slots * BLK, HD), bf),
            pltpu.VMEM((2, slots * BLK // min(ny, nz), HD), bf),
            pltpu.VMEM((slots * BLK // ny, HD), bf),
            pltpu.VMEM((slots * BLK // nz, HD), bf),
            pltpu.VMEM((slots * BLK, HD), bf),
            pltpu.VMEM((slots * BLK, HD), bf),
            pltpu.VMEM((heads, nx, 2 * part, HD), bf),
            pltpu.VMEM((8, NV * BLK), jnp.int32),
            pltpu.VMEM((tok // BLK, HD), jnp.int32),
            dma((5,)),
            dma((2,)),
            dma((2,)),
            dma((2, big)),
            dma((2, big)),
            dma((2, big)),
            dma((2, big)),
            dma((2, big)),
            dma((2, big)),
            dma((2, big)),
            dma((2, big)),
            dma((heads,)),
            dma((heads, nx, 2)),
            dma((heads, ntp)),
        ],
        compiler_params=pltpu.CompilerParams(
            collective_id=0, has_side_effects=True, vmem_limit_bytes=48 * 2**20
        ),
    )(vertical, slash, counts, queries, keys, values)


def solution(mesh):
    nseq, ntp = mesh.shape["seq"], mesh.shape["tp"]
    ny = 1 << ((nseq.bit_length() - 1 + 1) // 2)
    return jax.shard_map(
        functools.partial(per_device, nseq // ny, ny, ntp),
        mesh=mesh,
        in_specs=(P("seq", "tp"), P("seq", "tp"), P("seq", "tp"), P(), P(), P()),
        out_specs=P(("seq", "tp"), None),
        check_vma=False,
    )
```

```python
import functools
import math

import jax
import jax.numpy as jnp
from jax import lax
from jax.experimental import pallas as pl
from jax.experimental.pallas import tpu as pltpu
from jax.sharding import PartitionSpec as P

HD = 128
BLK = 64
NV = 8
NS = 2
SREACH = 8
HALO = SREACH * BLK

BIG = 1 << 30
NEG = -1e30
EXP2_SCALE = math.log2(math.e) / math.sqrt(HD)
MESH = pl.DeviceIdType.MESH


def attend_tile(row0, tile, head, slot0, refs):
    q_ref, wk, wv, kv, kpos_v, kpos_s, off_ref, seq0 = refs
    q = q_ref[pl.ds(row0, tile), pl.ds(pl.multiple_of(head * HD, HD), HD)]
    rows = lax.broadcasted_iota(jnp.int32, (tile, HD), 0) + (seq0 + row0)
    kt = (((1,), (1,)), ((), ()))
    vert_k = kv[pl.ds(slot0, NV), :BLK, :].reshape(NV * BLK, HD)
    vert_v = kv[pl.ds(slot0, NV), BLK:, :].reshape(NV * BLK, HD)
    sv = lax.dot_general(q, vert_k, kt, preferred_element_type=jnp.float32)
    pair = 2 * BLK
    r_i = lax.broadcasted_iota(jnp.int32, (pair, HD), 0)
    c_i = lax.broadcasted_iota(jnp.int32, (pair, HD), 1)
    straight = (r_i < BLK) == (c_i < BLK)
    off0, off1 = off_ref
    vals = []
    ss = []
    for p in range(tile // pair):
        start = row0 + p * pair + HALO
        s0 = start + off0 * -BLK
        s1 = start + off1 * -BLK
        s1b = s1 + BLK
        k2 = jnp.concatenate(
            [wk[pl.ds(s0, pair), :], wk[pl.ds(s1b, BLK), :], wk[pl.ds(s1, BLK), :]], axis=0
        )
        v2 = jnp.concatenate(
            [wv[pl.ds(s0, pair), :], wv[pl.ds(s1b, BLK), :], wv[pl.ds(s1, BLK), :]], axis=0
        )
        both = lax.dot_general(
            q[p * pair : (p + 1) * pair], k2, kt, preferred_element_type=jnp.float32
        )
        score = jnp.where(straight, both[:, :pair], both[:, pair:])
        block = (row0 + p * pair) // BLK
        kp0 = jnp.broadcast_to(kpos_s[pl.ds(block, 1), :], (BLK, HD))
        kp1 = jnp.broadcast_to(kpos_s[pl.ds(block + 1, 1), :], (BLK, HD))
        kp = jnp.concatenate([kp0, kp1], axis=0)
        ss.append(jnp.where(kp <= rows[p * pair : (p + 1) * pair], score, NEG))
        vals.append(v2)
    ss = jnp.concatenate(ss, axis=0)
    parts = []
    for k in range(NV * BLK // HD):
        kp = kpos_v[0:1, k * HD : (k + 1) * HD]
        parts.append(jnp.where(kp <= rows, sv[:, k * HD : (k + 1) * HD], NEG))
    top = ss
    for part in parts:
        top = jnp.maximum(top, part)
    top = jnp.max(top, axis=1, keepdims=True)
    ps = jnp.exp2((ss - top) * EXP2_SCALE)
    total = ps
    probs = []
    for part in parts:
        prob = jnp.exp2((part - top) * EXP2_SCALE)
        total = total + prob
        probs.append(prob.astype(jnp.bfloat16))
    total = jnp.sum(total, axis=1, keepdims=True)
    acc = jnp.dot(
        jnp.concatenate(probs, axis=1), vert_v, preferred_element_type=jnp.float32
    )
    slash_acc = []
    for p in range(tile // pair):
        w = ps[p * pair : (p + 1) * pair]
        w2 = jnp.concatenate(
            [
                jnp.where(straight, w, 0.0).astype(jnp.bfloat16),
                jnp.where(straight, 0.0, w).astype(jnp.bfloat16),
            ],
            axis=1,
        )
        slash_acc.append(jnp.dot(w2, vals[p], preferred_element_type=jnp.float32))
    acc = acc + jnp.concatenate(slash_acc, axis=0)
    return (acc / total).astype(jnp.bfloat16)


def key_positions(head, seq, blocks_dev, vert, slash, counts, kpos_v, kpos_s):
    n_vert = counts[0, head]
    n_slash = counts[1, head]
    lane = lax.broadcasted_iota(jnp.int32, (8, HD), 1)
    for k in range(NV // 2):
        pos = jnp.where(lane < BLK, vert[2 * k, head], vert[2 * k + 1, head]) * BLK + lane % BLK
        used = jnp.where(lane < BLK, 2 * k, 2 * k + 1) < n_vert
        kpos_v[:, k * HD : (k + 1) * HD] = jnp.where(used, pos, BIG)
    row = lax.broadcasted_iota(jnp.int32, (blocks_dev, HD), 0)
    col = lax.broadcasted_iota(jnp.int32, (blocks_dev, HD), 1)
    first = (row % 2 == 0) == (col < BLK)
    block = seq * blocks_dev + row - jnp.where(first, slash[0, head], slash[1, head])
    dead = (block < 0) | (jnp.where(first, 0, 1) >= n_slash)
    for j in range(NV):
        dead = dead | ((block == vert[j, head]) & (jnp.full_like(row, j) < n_vert))
    kpos_s[...] = jnp.where(dead, BIG, block * BLK + col % BLK)


def fused(
    nz, ny, ntp, packed,
    vert, slash, counts, piece_at, second_at, pack, q_hbm, k_hbm, v_hbm, out,
    q_ref, wk, wv, hk, hv, snd, got1k, got1v, mid, got2k, got2v, col, kv,
    obuf, obox, kpos_v, kpos_s,
    local_sem, halo_send, halo_recv, send1, recv1, send2, recv2, send3, recv3, send4, recv4,
    own_sem, out_send, out_recv, place_sem,
):
    tok = q_ref.shape[0]
    heads = q_ref.shape[1] // HD
    blocks_dev = tok // BLK
    half = heads * NV // 2
    quad = NV // 2
    seq = lax.axis_index("seq")
    tp = lax.axis_index("tp")
    z, y = seq // ny, seq % ny
    nseq = nz * ny
    axes = ((ny, nz), (nz, ny))
    mine = ((y, z), (z, y))
    got1, got2 = (got1k, got1v), (got2k, got2v)

    def at(side, first, second):
        return (second * ny + first if side == 0 else first * ny + second, tp)

    def local(i, src, dst):
        return pltpu.make_async_copy(src, dst, local_sem.at[i])

    copies = [
        local(0, k_hbm, wk.at[HALO:]),
        local(1, v_hbm, wv.at[HALO:]),
        local(2, q_hbm, q_ref),
    ]
    for c in copies:
        c.start()

    barrier = pltpu.get_barrier_semaphore()

    @pl.loop(1, ny)
    def _(d):
        peer = z * ny + lax.rem(y + d, ny)
        pl.semaphore_signal(barrier, inc=1, device_id=(peer, tp), device_id_type=MESH)

    @pl.loop(1, nz)
    def _(d):
        peer = lax.rem(z + d, nz) * ny + y
        pl.semaphore_signal(barrier, inc=1, device_id=(peer, tp), device_id_type=MESH)

    @pl.loop(1, ntp)
    def _(d):
        pl.semaphore_signal(
            barrier, inc=1, device_id=(seq, lax.rem(tp + d, ntp)), device_id_type=MESH
        )

    after, before = lax.rem(seq + 1, nseq), lax.rem(seq + nseq - 1, nseq)
    for peer in (after, before):
        pl.semaphore_signal(barrier, inc=1, device_id=(peer, tp), device_id_type=MESH)

    copies[0].wait()
    copies[1].wait()

    for side in (0, 1):
        n = axes[side][0]
        piece = 2 * BLK // n

        @pl.loop(0, packed)
        def _(k, side=side, n=n, piece=piece):
            if packed < half:
                inside = pack[side, k]
            else:
                inside = pack[side * quad + k % quad, tp * heads + k // quad]
            row = inside * BLK + HALO
            rows_k = wk[pl.ds(row, BLK), :]
            rows_v = wv[pl.ds(row, BLK), :]
            for c in range(n):
                rows, at_row = (rows_k, c * piece) if c < n // 2 else (rows_v, c * piece - BLK)
                snd[side, c, k] = rows[at_row : at_row + piece]

    pl.semaphore_wait(barrier, ny + nz + ntp - 3 + 2)

    halo = [
        pltpu.make_async_remote_copy(
            src_ref=w.at[tok : tok + HALO],
            dst_ref=dst,
            send_sem=halo_send.at[i],
            recv_sem=halo_recv.at[i],
            device_id=(after, tp),
            device_id_type=MESH,
        )
        for i, (w, dst) in enumerate(((wk, hk), (wv, hv)))
    ]

    def spread1(side, d):
        n, me = axes[side][0], mine[side][0]
        peer = lax.rem(me + d, n)
        return pltpu.make_async_remote_copy(
            src_ref=snd.at[side, peer],
            dst_ref=got1[side].at[pl.ds(me * packed, packed)],
            send_sem=send1.at[side, d],
            recv_sem=recv1.at[side, n - d],
            device_id=at(side, peer, mine[side][1]),
            device_id_type=MESH,
        )

    def spread2(side, d):
        n, me = axes[side][1], mine[side][1]
        share = half // n
        peer = lax.rem(me + d, n)
        return pltpu.make_async_remote_copy(
            src_ref=mid.at[side, pl.ds(peer * share, share)],
            dst_ref=got2[side].at[pl.ds(me * share, share)],
            send_sem=send2.at[side, d],
            recv_sem=recv2.at[side, n - d],
            device_id=at(side, mine[side][0], peer),
            device_id_type=MESH,
        )

    def gather2(side, d):
        n, me = axes[side][1], mine[side][1]
        share = half // n
        place = col.at[side, pl.ds(me * share, share)]
        return pltpu.make_async_remote_copy(
            src_ref=place,
            dst_ref=place,
            send_sem=send3.at[side, d],
            recv_sem=recv3.at[side, n - d],
            device_id=at(side, mine[side][0], lax.rem(me + d, n)),
            device_id_type=MESH,
        )

    def rows_of(side):
        n, me = axes[side][0], mine[side][0]
        piece = 2 * BLK // n
        return pl.ds(pl.multiple_of(me * piece, 16), piece)

    def gather1(h, side, d):
        n, me = axes[side][0], mine[side][0]
        return pltpu.make_async_remote_copy(
            src_ref=col.at[side, pl.ds(h * quad, quad)],
            dst_ref=kv.at[pl.ds(h * NV + side * quad, quad), rows_of(side)],
            send_sem=send4.at[h, side, d],
            recv_sem=recv4.at[h, side, n - d],
            device_id=at(side, lax.rem(me + d, n), mine[side][1]),
            device_id_type=MESH,
        )

    def each(side, axis, step):
        @pl.loop(1, axes[side][axis])
        def _(d):
            step(d)

    for side in (0, 1):
        each(side, 0, lambda d, side=side: spread1(side, d).start())
    for c in halo:
        c.start()

    for side in (0, 1):
        me = mine[side][0]
        got1[side][pl.ds(me * packed, packed)] = snd[side, me]
        each(side, 0, lambda d, side=side: spread1(side, d).wait_recv())

        @pl.loop(0, half)
        def _(i, side=side):
            mid[side, i] = got1[side][piece_at[side * quad + i % quad, tp * heads + i // quad]]

        each(side, 1, lambda d, side=side: spread2(side, d).start())

    for side in (0, 1):
        n, me = axes[side][1], mine[side][1]
        share = half // n
        got2[side][pl.ds(me * share, share)] = mid[side, pl.ds(me * share, share)]
        each(side, 1, lambda d, side=side: spread2(side, d).wait_recv())
        for r in range(share):
            i = me * share + r
            second = second_at[side * quad + i % quad, tp * heads + i // quad]
            col[side, i] = got2[side][second * share + r]
        each(side, 1, lambda d, side=side: gather2(side, d).start())

    def start_head(h):
        for side in (0, 1):
            each(side, 0, lambda d, side=side: gather1(h, side, d).start())

    def own_head(h):
        for side in (0, 1):
            kv[pl.ds(h * NV + side * quad, quad), rows_of(side)] = col[side, pl.ds(h * quad, quad)]

    for side in (0, 1):
        each(side, 1, lambda d, side=side: gather2(side, d).wait_recv())
        each(side, 0, lambda d, side=side: gather1(0, side, d).start())
    start_head(1)

    for c in halo:
        c.wait_recv()
    joins = [local(3, hk, wk.at[0:HALO]), local(4, hv, wv.at[0:HALO])]
    for c in joins:
        c.start()
    copies[2].wait()
    for c in joins:
        c.wait()

    nx = ntp // 2
    part = tok // ntp
    tile = 2 * part
    x, core = tp // 2, lax.rem(tp, 2)
    order = (2, 1, 3, 0) if nx == 4 else tuple(range(nx - 1, -1, -1))

    def send_out(h, j, c, target):
        src = pl.multiple_of(c * part, 16)
        return pltpu.make_async_remote_copy(
            src_ref=obuf.at[h, j, pl.ds(src, part), :],
            dst_ref=obox.at[tp, h],
            send_sem=out_send.at[h, j, c],
            recv_sem=out_recv.at[h, tp],
            device_id=(seq, target),
            device_id_type=MESH,
        )

    def keep_out(h, j):
        src = pl.multiple_of(core * part, 16)
        cols = pl.ds(pl.multiple_of((tp * heads + h) * HD, HD), HD)
        return pltpu.make_async_copy(
            obuf.at[h, j, pl.ds(src, part), :], out.at[:, cols], own_sem.at[h]
        )

    def place_out(h, source):
        cols = pl.ds(pl.multiple_of((source * heads + h) * HD, HD), HD)
        return pltpu.make_async_copy(obox.at[source, h], out.at[:, cols], place_sem.at[source, h])

    def landed(h, source):
        return pltpu.make_async_remote_copy(
            src_ref=obuf.at[h, 0, pl.ds(0, part), :],
            dst_ref=obox.at[source, h],
            send_sem=out_send.at[h, 0, 0],
            recv_sem=out_recv.at[h, source],
            device_id=(seq, source),
            device_id_type=MESH,
        )

    @pl.loop(0, heads)
    def _(h):
        head = tp * heads + h
        key_positions(head, seq, blocks_dev, vert, slash, counts, kpos_v, kpos_s)
        own_head(h)
        for side in (0, 1):
            each(side, 0, lambda d, side=side: gather1(h, side, d).wait_recv())
        refs = (
            q_ref, wk, wv, kv, kpos_v, kpos_s,
            (slash[0, head], slash[1, head]), seq * tok,
        )
        for j, step in enumerate(order):
            chip = lax.rem(x + step, nx)
            row0 = pl.multiple_of(chip * tile, BLK)
            obuf[h, j] = attend_tile(row0, tile, h, h * NV, refs)
            if step:
                for c in (0, 1):
                    send_out(h, j, c, chip * 2 + c).start()
            else:
                send_out(h, j, 1 - core, chip * 2 + 1 - core).start()
                keep_out(h, j).start()
            if j == 0:

                @pl.when(h < heads - 2)
                def _():
                    start_head(h + 2)

    @pl.loop(0, heads)
    def _(h):
        @pl.loop(1, ntp)
        def _(d):
            source = lax.rem(tp + d, ntp)
            landed(h, source).wait_recv()
            place_out(h, source).start()

    @pl.loop(0, heads)
    def _(h):
        @pl.loop(1, ntp)
        def _(d):
            place_out(h, lax.rem(tp + d, ntp)).wait()

        keep_out(h, nx - 1).wait()
        for j, step in enumerate(order):
            chip = lax.rem(x + step, nx)
            if step:
                for c in (0, 1):
                    send_out(h, j, c, chip * 2 + c).wait_send()
            else:
                send_out(h, j, 1 - core, chip * 2 + 1 - core).wait_send()

    for c in halo:
        c.wait_send()
    for side in (0, 1):
        each(side, 0, lambda d, side=side: spread1(side, d).wait_send())
        each(side, 1, lambda d, side=side: spread2(side, d).wait_send())
        each(side, 1, lambda d, side=side: gather2(side, d).wait_send())

    @pl.loop(0, heads)
    def _(h):
        for side in (0, 1):
            each(side, 0, lambda d, side=side: gather1(h, side, d).wait_send())


def attend(nz, ny, ntp, packed, lists, tables, queries, keys, values):
    tok, width = queries.shape
    heads = width // HD
    half = heads * NV // 2
    part = tok // ntp
    nx = ntp // 2
    big = max(ny, nz)
    pieces = [2 * BLK // n for n in (ny, nz)]
    dma = pltpu.SemaphoreType.DMA
    bf = jnp.bfloat16
    smem = pl.BlockSpec(memory_space=pltpu.SMEM)
    hbm = pl.BlockSpec(memory_space=pltpu.HBM)
    return pl.pallas_call(
        functools.partial(fused, nz, ny, ntp, packed),
        out_shape=jax.ShapeDtypeStruct((part, width * ntp), bf),
        in_specs=[smem] * 6 + [hbm] * 3,
        out_specs=pl.BlockSpec(memory_space=pl.ANY),
        scratch_shapes=[
            pltpu.VMEM((tok, width), bf),
            pltpu.VMEM((HALO + tok, HD), bf),
            pltpu.VMEM((HALO + tok, HD), bf),
            pltpu.VMEM((HALO, HD), bf),
            pltpu.VMEM((HALO, HD), bf),
            pltpu.VMEM((2, big, packed, pieces[0], HD), bf),
            pltpu.VMEM((ny * packed, pieces[0], HD), bf),
            pltpu.VMEM((nz * packed, pieces[1], HD), bf),
            pltpu.VMEM((2, half, pieces[0], HD), bf),
            pltpu.VMEM((half, pieces[0], HD), bf),
            pltpu.VMEM((half, pieces[1], HD), bf),
            pltpu.VMEM((2, half, pieces[0], HD), bf),
            pltpu.VMEM((heads * NV, 2 * BLK, HD), bf),
            pltpu.VMEM((heads, nx, 2 * part, HD), bf),
            pltpu.VMEM((ntp, heads, part, HD), bf),
            pltpu.VMEM((8, NV * BLK), jnp.int32),
            pltpu.VMEM((tok // BLK, HD), jnp.int32),
            dma((5,)),
            dma((2,)),
            dma((2,)),
            dma((2, big)),
            dma((2, big)),
            dma((2, big)),
            dma((2, big)),
            dma((2, big)),
            dma((2, big)),
            dma((heads, 2, big)),
            dma((heads, 2, big)),
            dma((heads,)),
            dma((heads, nx, 2)),
            dma((heads, ntp)),
            dma((ntp, heads)),
        ],
        compiler_params=pltpu.CompilerParams(
            collective_id=0 if packed < half else 1,
            has_side_effects=True,
            vmem_limit_bytes=60 * 2**20,
        ),
    )(*lists, *tables, queries, keys, values)


FEW = 3
CODE = 32


def plan(nz, ny, heads, blocks_dev, vert, counts, few_at, all_at, second_at, inside_at, pack, few, wide, wide_n):
    groups_heads = vert.shape[1]
    seq, tp = lax.axis_index("seq"), lax.axis_index("tp")
    wide[...] = jnp.zeros_like(wide)
    wide_n[...] = jnp.zeros_like(wide_n)
    wide[:, :groups_heads] = vert[...]
    wide_n[:, :groups_heads] = jnp.broadcast_to(counts[0:1, :], (NV, groups_heads))
    block = wide[...]
    quad = NV // 2
    slot = lax.broadcasted_iota(jnp.int32, block.shape, 0)
    lane = lax.broadcasted_iota(jnp.int32, block.shape, 1)
    j, h = slot % quad, lane % heads
    order = h * quad + j

    def split(a, by):
        q = ((a.astype(jnp.float32) + 0.5) * (1.0 / by)).astype(jnp.int32)
        return q, a - q * by

    device, inside = split(block, blocks_dev)
    dev_z, dev_y = split(device, ny)
    wanted = (slot < wide_n[...]) & ((slot > 0) | (h == 0))
    owner = jnp.where(wanted, device, -1 - order)
    rank = jnp.zeros_like(block)
    for dh in range(heads):
        moved = pltpu.roll(owner, dh, 1) if dh else owner
        for dj in range(1 - quad, quad if dh else 0):
            other = pltpu.roll(moved, (NV - dj) % NV, 0) if dj else moved
            here = (h >= dh) & (j + dj >= 0) & (j + dj < quad) & (other == owner)
            rank = rank + here.astype(jnp.int32)
    first = jnp.where(slot < quad, dev_y, dev_z)
    few_at[...] = first * FEW + jnp.minimum(rank, FEW - 1)
    all_at[...] = first * (heads * quad) + order
    second_at[...] = jnp.where(slot < quad, dev_z, dev_y)
    inside_at[...] = inside
    most = jnp.max(jnp.where(lane < groups_heads, rank, 0))
    few[0] = (most < FEW).astype(jnp.int32)
    hit = wanted & (owner == seq) & (lane >= tp * heads) & (lane < tp * heads + heads)
    place = jnp.where(rank == 0, 1, jnp.where(rank == 1, CODE, CODE * CODE))
    coded = jnp.where(hit & (rank < FEW), inside * place, 0)
    for side in (0, 1):
        total = jnp.sum(jnp.where((slot < quad) == (side == 0), coded, 0))
        for k in range(FEW):
            pack[side, k] = total & (CODE - 1)
            total = total >> 5


def per_device(nz, ny, ntp, queries, keys, values, vertical, slash, counts):
    tok, width = queries.shape
    heads = width // HD
    bf_lists = (vertical.T, slash.T, counts.T)
    wide = jax.ShapeDtypeStruct((NV, HD), jnp.int32)
    smem = pl.BlockSpec(memory_space=pltpu.SMEM)
    vmem = pl.BlockSpec(memory_space=pltpu.VMEM)
    few_at, all_at, second_at, inside_at, pack, few = pl.pallas_call(
        functools.partial(plan, nz, ny, heads, tok // BLK),
        out_shape=(wide,) * 4
        + (jax.ShapeDtypeStruct((2, FEW), jnp.int32), jax.ShapeDtypeStruct((1,), jnp.int32)),
        in_specs=[vmem, vmem],
        out_specs=(vmem,) * 4 + (smem, smem),
        scratch_shapes=[pltpu.VMEM((NV, HD), jnp.int32), pltpu.VMEM((NV, HD), jnp.int32)],
    )(bf_lists[0], bf_lists[2])

    def sparse(few_at, all_at, second_at, inside_at, pack, *args):
        return attend(nz, ny, ntp, FEW, bf_lists, (few_at, second_at, pack), *args)

    def dense(few_at, all_at, second_at, inside_at, pack, *args):
        half = heads * NV // 2
        return attend(nz, ny, ntp, half, bf_lists, (all_at, second_at, inside_at), *args)

    return lax.cond(
        few[0] > 0, sparse, dense, few_at, all_at, second_at, inside_at, pack, queries, keys, values
    )


def solution(mesh):
    nseq, ntp = mesh.shape["seq"], mesh.shape["tp"]
    ny = 1 << ((nseq.bit_length() - 1 + 1) // 2)
    return jax.shard_map(
        functools.partial(per_device, nseq // ny, ny, ntp),
        mesh=mesh,
        in_specs=(P("seq", "tp"), P("seq", "tp"), P("seq", "tp"), P(), P(), P()),
        out_specs=P(("seq", "tp"), None),
        check_vma=False,
    )
```

```python
import functools
import math

import jax
import jax.numpy as jnp
from jax import lax
from jax.experimental import pallas as pl
from jax.experimental.pallas import tpu as pltpu
from jax.sharding import PartitionSpec as P

HD = 128
BLK = 64
NV = 8
NS = 2
SREACH = 8
HALO = SREACH * BLK

BIG = 1 << 30
NEG = -1e30
EXP2_SCALE = math.log2(math.e) / math.sqrt(HD)
MESH = pl.DeviceIdType.MESH


def attend_tile(row0, tile, head, slot0, refs):
    q_ref, wk, wv, kv, kpos_v, kpos_s, off_ref, seq0 = refs
    q = q_ref[pl.ds(row0, tile), pl.ds(pl.multiple_of(head * HD, HD), HD)]
    rows = lax.broadcasted_iota(jnp.int32, (tile, HD), 0) + (seq0 + row0)
    kt = (((1,), (1,)), ((), ()))
    rest = (NV - 1) * BLK
    vert_k = jnp.concatenate([kv[0, :BLK], kv[pl.ds(slot0, NV - 1), :BLK].reshape(rest, HD)], axis=0)
    vert_v = jnp.concatenate([kv[0, BLK:], kv[pl.ds(slot0, NV - 1), BLK:].reshape(rest, HD)], axis=0)
    sv = lax.dot_general(q, vert_k, kt, preferred_element_type=jnp.float32)
    pair = 2 * BLK
    r_i = lax.broadcasted_iota(jnp.int32, (pair, HD), 0)
    c_i = lax.broadcasted_iota(jnp.int32, (pair, HD), 1)
    straight = (r_i < BLK) == (c_i < BLK)
    off0, off1 = off_ref
    vals = []
    ss = []
    for p in range(tile // pair):
        start = row0 + p * pair + HALO
        s0 = start + off0 * -BLK
        s1 = start + off1 * -BLK
        s1b = s1 + BLK
        k2 = jnp.concatenate(
            [wk[pl.ds(s0, pair), :], wk[pl.ds(s1b, BLK), :], wk[pl.ds(s1, BLK), :]], axis=0
        )
        v2 = jnp.concatenate(
            [wv[pl.ds(s0, pair), :], wv[pl.ds(s1b, BLK), :], wv[pl.ds(s1, BLK), :]], axis=0
        )
        both = lax.dot_general(
            q[p * pair : (p + 1) * pair], k2, kt, preferred_element_type=jnp.float32
        )
        score = jnp.where(straight, both[:, :pair], both[:, pair:])
        block = (row0 + p * pair) // BLK
        kp0 = jnp.broadcast_to(kpos_s[pl.ds(block, 1), :], (BLK, HD))
        kp1 = jnp.broadcast_to(kpos_s[pl.ds(block + 1, 1), :], (BLK, HD))
        kp = jnp.concatenate([kp0, kp1], axis=0)
        ss.append(jnp.where(kp <= rows[p * pair : (p + 1) * pair], score, NEG))
        vals.append(v2)
    ss = jnp.concatenate(ss, axis=0)
    parts = []
    for k in range(NV * BLK // HD):
        kp = kpos_v[0:1, k * HD : (k + 1) * HD]
        parts.append(jnp.where(kp <= rows, sv[:, k * HD : (k + 1) * HD], NEG))
    top = ss
    for part in parts:
        top = jnp.maximum(top, part)
    top = jnp.max(top, axis=1, keepdims=True)
    ps = jnp.exp2((ss - top) * EXP2_SCALE)
    total = ps
    probs = []
    for part in parts:
        prob = jnp.exp2((part - top) * EXP2_SCALE)
        total = total + prob
        probs.append(prob.astype(jnp.bfloat16))
    total = jnp.sum(total, axis=1, keepdims=True)
    acc = jnp.dot(
        jnp.concatenate(probs, axis=1), vert_v, preferred_element_type=jnp.float32
    )
    slash_acc = []
    for p in range(tile // pair):
        w = ps[p * pair : (p + 1) * pair]
        w2 = jnp.concatenate(
            [
                jnp.where(straight, w, 0.0).astype(jnp.bfloat16),
                jnp.where(straight, 0.0, w).astype(jnp.bfloat16),
            ],
            axis=1,
        )
        slash_acc.append(jnp.dot(w2, vals[p], preferred_element_type=jnp.float32))
    acc = acc + jnp.concatenate(slash_acc, axis=0)
    return (acc / total).astype(jnp.bfloat16)


def key_positions(head, seq, blocks_dev, vert, slash, counts, kpos_v, kpos_s):
    n_vert = counts[0, head]
    n_slash = counts[1, head]
    lane = lax.broadcasted_iota(jnp.int32, (8, HD), 1)
    for k in range(NV // 2):
        pos = jnp.where(lane < BLK, vert[2 * k, head], vert[2 * k + 1, head]) * BLK + lane % BLK
        used = jnp.where(lane < BLK, 2 * k, 2 * k + 1) < n_vert
        kpos_v[:, k * HD : (k + 1) * HD] = jnp.where(used, pos, BIG)
    row = lax.broadcasted_iota(jnp.int32, (blocks_dev, HD), 0)
    col = lax.broadcasted_iota(jnp.int32, (blocks_dev, HD), 1)
    first = (row % 2 == 0) == (col < BLK)
    block = seq * blocks_dev + row - jnp.where(first, slash[0, head], slash[1, head])
    dead = (block < 0) | (jnp.where(first, 0, 1) >= n_slash)
    for j in range(NV):
        dead = dead | ((block == vert[j, head]) & (jnp.full_like(row, j) < n_vert))
    kpos_s[...] = jnp.where(dead, BIG, block * BLK + col % BLK)


def fused(
    nz, ny, ntp, slots, packed, row_packed,
    vert, slash, counts, pack, row_pack, slot_at, starts, q_hbm, k_hbm, v_hbm, out,
    q_ref, wk, wv, hk, hv, snd, got1k, got1v, mid, got2k, got2v, col, kv,
    obuf, obox, kpos_v, kpos_s,
    local_sem, halo_send, halo_recv, send1, recv1, send2, recv2, send3, recv3,
    own_sem, out_send, out_recv, place_sem,
):
    tok = q_ref.shape[0]
    heads = q_ref.shape[1] // HD
    blocks_dev = tok // BLK
    half = slots // 2
    quad = NV // 2
    seq = lax.axis_index("seq")
    tp = lax.axis_index("tp")
    z, y = seq // ny, lax.rem(seq, ny)
    nseq = nz * ny
    axes = ((ny, nz), (nz, ny))
    mine = ((y, z), (z, y))
    got1, got2 = (got1k, got1v), (got2k, got2v)

    def at(side, first, second):
        return (second * ny + first if side == 0 else first * ny + second, tp)

    def local(i, src, dst):
        return pltpu.make_async_copy(src, dst, local_sem.at[i])

    copies = [
        local(0, k_hbm, wk.at[HALO:]),
        local(1, v_hbm, wv.at[HALO:]),
        local(2, q_hbm, q_ref),
    ]
    for c in copies:
        c.start()

    barrier = pltpu.get_barrier_semaphore()

    for d in range(1, ny):
        peer = z * ny + lax.rem(y + d, ny)
        pl.semaphore_signal(barrier, inc=1, device_id=(peer, tp), device_id_type=MESH)
    for d in range(1, nz):
        peer = lax.rem(z + d, nz) * ny + y
        pl.semaphore_signal(barrier, inc=1, device_id=(peer, tp), device_id_type=MESH)
    for d in range(1, ntp):
        pl.semaphore_signal(
            barrier, inc=1, device_id=(seq, lax.rem(tp + d, ntp)), device_id_type=MESH
        )

    after, before = lax.rem(seq + 1, nseq), lax.rem(seq + nseq - 1, nseq)
    for peer in (after, before):
        pl.semaphore_signal(barrier, inc=1, device_id=(peer, tp), device_id_type=MESH)

    kv[slots:] = jnp.zeros_like(kv[slots:])
    copies[0].wait()
    copies[1].wait()

    for side in (0, 1):
        n = axes[side][0]
        piece = 2 * BLK // n

        @pl.loop(0, packed)
        def _(k, side=side, n=n, piece=piece):
            row = pack[side, k] * BLK + HALO
            rows_k = wk[pl.ds(row, BLK), :]
            rows_v = wv[pl.ds(row, BLK), :]
            for c in range(n):
                rows, at_row = (rows_k, c * piece) if c < n // 2 else (rows_v, c * piece - BLK)
                snd[side, c, k] = rows[at_row : at_row + piece]

    pl.semaphore_wait(barrier, ny + nz + ntp - 3 + 2)

    halo = [
        pltpu.make_async_remote_copy(
            src_ref=w.at[tok : tok + HALO],
            dst_ref=dst,
            send_sem=halo_send.at[i],
            recv_sem=halo_recv.at[i],
            device_id=(after, tp),
            device_id_type=MESH,
        )
        for i, (w, dst) in enumerate(((wk, hk), (wv, hv)))
    ]

    def spread1(side, d):
        n, me = axes[side][0], mine[side][0]
        peer = lax.rem(me + d, n)
        return pltpu.make_async_remote_copy(
            src_ref=snd.at[side, peer],
            dst_ref=got1[side].at[pl.ds(me * packed, packed)],
            send_sem=send1.at[side, d],
            recv_sem=recv1.at[side, n - d],
            device_id=at(side, peer, mine[side][1]),
            device_id_type=MESH,
        )

    def gather2(side, d):
        n, me = axes[side][1], mine[side][1]
        peer = lax.rem(me + d, n)
        return pltpu.make_async_remote_copy(
            src_ref=mid.at[side],
            dst_ref=got2[side].at[pl.ds(me * row_packed, row_packed)],
            send_sem=send2.at[side, d],
            recv_sem=recv2.at[side, n - d],
            device_id=at(side, mine[side][0], peer),
            device_id_type=MESH,
        )

    def rows_of(side):
        n, me = axes[side][0], mine[side][0]
        piece = 2 * BLK // n
        return pl.ds(pl.multiple_of(me * piece, 16), piece)

    more = half - quad

    def parts(chunk, side):
        if chunk == 0:
            return pl.ds(0, quad), pl.ds(side * quad, quad)
        return pl.ds(quad, more), pl.ds(NV + side * more, more)

    def gather1(chunk, side, d):
        n, me = axes[side][0], mine[side][0]
        src, dst = parts(chunk, side)
        return pltpu.make_async_remote_copy(
            src_ref=col.at[side, src],
            dst_ref=kv.at[dst, rows_of(side)],
            send_sem=send3.at[chunk, side, d],
            recv_sem=recv3.at[chunk, side, n - d],
            device_id=at(side, lax.rem(me + d, n), mine[side][1]),
            device_id_type=MESH,
        )

    def far_first(n):
        return sorted(range(1, n), key=lambda d: -min(d, n - d))

    def each(axis, step):
        for d in far_first(max(ny, nz)):
            for side in (0, 1):
                if d < axes[side][axis]:
                    step(side, d)

    each(0, lambda side, d: spread1(side, d).start())
    halo[0].start()

    for side in (0, 1):
        me = mine[side][0]
        got1[side][pl.ds(me * packed, packed)] = snd[side, me]
    for side in (0, 1):
        for d in range(1, axes[side][0]):
            spread1(side, d).wait_recv()
        for k in range(row_packed):
            mid[side, k] = got1[side][row_pack[side, k]]
        for d in far_first(axes[side][1]):
            gather2(side, d).start()
    halo[1].start()

    for side in (0, 1):
        me = mine[side][1]
        got2[side][pl.ds(me * row_packed, row_packed)] = mid[side]
    for side in (0, 1):
        for d in range(1, axes[side][1]):
            gather2(side, d).wait_recv()
        for i in range(half):
            col[side, i] = got2[side][slot_at[side, i]]
        for d in far_first(axes[side][0]):
            gather1(0, side, d).start()
    each(0, lambda side, d: gather1(1, side, d).start())
    for chunk in (0, 1):
        for side in (0, 1):
            src, dst = parts(chunk, side)
            kv[dst, rows_of(side)] = col[side, src]

    for c in halo:
        c.wait_recv()
    joins = [local(3, hk, wk.at[0:HALO]), local(4, hv, wv.at[0:HALO])]
    for c in joins:
        c.start()
    copies[2].wait()
    for c in joins:
        c.wait()

    nx = ntp // 2
    part = tok // ntp
    tile = 2 * part
    x, core = tp // 2, lax.rem(tp, 2)
    order = (2, 1, 3, 0) if nx == 4 else tuple(range(nx - 1, -1, -1))

    def send_out(h, j, c, target):
        src = pl.multiple_of(c * part, 16)
        return pltpu.make_async_remote_copy(
            src_ref=obuf.at[h, j, pl.ds(src, part), :],
            dst_ref=obox.at[tp, h],
            send_sem=out_send.at[h, j, c],
            recv_sem=out_recv.at[h, tp],
            device_id=(seq, target),
            device_id_type=MESH,
        )

    def keep_out(h, j):
        src = pl.multiple_of(core * part, 16)
        cols = pl.ds(pl.multiple_of((tp * heads + h) * HD, HD), HD)
        return pltpu.make_async_copy(
            obuf.at[h, j, pl.ds(src, part), :], out.at[:, cols], own_sem.at[h]
        )

    def place_out(h, source):
        cols = pl.ds(pl.multiple_of((source * heads + h) * HD, HD), HD)
        return pltpu.make_async_copy(obox.at[source, h], out.at[:, cols], place_sem.at[source, h])

    def landed(h, source):
        return pltpu.make_async_remote_copy(
            src_ref=obuf.at[h, 0, pl.ds(0, part), :],
            dst_ref=obox.at[source, h],
            send_sem=out_send.at[h, 0, 0],
            recv_sem=out_recv.at[h, source],
            device_id=(seq, source),
            device_id_type=MESH,
        )

    def run_head(h, slot0):
        head = tp * heads + h
        key_positions(head, seq, blocks_dev, vert, slash, counts, kpos_v, kpos_s)
        if isinstance(h, int):
            each(0, lambda side, d: gather1(0, side, d).wait_recv())
        refs = (
            q_ref, wk, wv, kv, kpos_v, kpos_s,
            (slash[0, head], slash[1, head]), seq * tok,
        )
        for j, step in enumerate(order):
            chip = lax.rem(x + step, nx)
            row0 = pl.multiple_of(chip * tile, BLK)
            obuf[h, j] = attend_tile(row0, tile, h, slot0, refs)
            if step:
                for c in (0, 1):
                    send_out(h, j, c, chip * 2 + c).start()
            else:
                send_out(h, j, 1 - core, chip * 2 + 1 - core).start()
                keep_out(h, j).start()

    run_head(0, 1)
    each(0, lambda side, d: gather1(1, side, d).wait_recv())

    @pl.loop(1, heads)
    def _(h):
        run_head(h, starts[h])

    @pl.loop(0, heads)
    def _(h):
        @pl.loop(1, ntp)
        def _(d):
            source = lax.rem(tp + d, ntp)
            landed(h, source).wait_recv()
            place_out(h, source).start()

    @pl.loop(0, heads)
    def _(h):
        @pl.loop(1, ntp)
        def _(d):
            place_out(h, lax.rem(tp + d, ntp)).wait()

        keep_out(h, nx - 1).wait()
        for j, step in enumerate(order):
            chip = lax.rem(x + step, nx)
            if step:
                for c in (0, 1):
                    send_out(h, j, c, chip * 2 + c).wait_send()
            else:
                send_out(h, j, 1 - core, chip * 2 + 1 - core).wait_send()

    for c in halo:
        c.wait_send()
    each(0, lambda side, d: spread1(side, d).wait_send())
    each(1, lambda side, d: gather2(side, d).wait_send())
    for chunk in (0, 1):
        each(0, lambda side, d: gather1(chunk, side, d).wait_send())


def attend(nz, ny, ntp, slots, packed, row_packed, lists, tables, queries, keys, values):
    tok, width = queries.shape
    heads = width // HD
    part = tok // ntp
    nx = ntp // 2
    big = max(ny, nz)
    half = slots // 2
    pieces = [2 * BLK // n for n in (ny, nz)]
    dma = pltpu.SemaphoreType.DMA
    bf = jnp.bfloat16
    smem = pl.BlockSpec(memory_space=pltpu.SMEM)
    hbm = pl.BlockSpec(memory_space=pltpu.HBM)
    return pl.pallas_call(
        functools.partial(fused, nz, ny, ntp, slots, packed, row_packed),
        out_shape=jax.ShapeDtypeStruct((part, width * ntp), bf),
        in_specs=[smem] * 7 + [hbm] * 3,
        out_specs=pl.BlockSpec(memory_space=pl.ANY),
        scratch_shapes=[
            pltpu.VMEM((tok, width), bf),
            pltpu.VMEM((HALO + tok, HD), bf),
            pltpu.VMEM((HALO + tok, HD), bf),
            pltpu.VMEM((HALO, HD), bf),
            pltpu.VMEM((HALO, HD), bf),
            pltpu.VMEM((2, big, packed, pieces[0], HD), bf),
            pltpu.VMEM((ny * packed, pieces[0], HD), bf),
            pltpu.VMEM((nz * packed, pieces[1], HD), bf),
            pltpu.VMEM((2, row_packed, pieces[0], HD), bf),
            pltpu.VMEM((nz * row_packed, pieces[0], HD), bf),
            pltpu.VMEM((ny * row_packed, pieces[1], HD), bf),
            pltpu.VMEM((2, half, pieces[0], HD), bf),
            pltpu.VMEM((slots + NV, 2 * BLK, HD), bf),
            pltpu.VMEM((heads, nx, 2 * part, HD), bf),
            pltpu.VMEM((ntp, heads, part, HD), bf),
            pltpu.VMEM((8, NV * BLK), jnp.int32),
            pltpu.VMEM((tok // BLK, HD), jnp.int32),
            dma((5,)),
            dma((2,)),
            dma((2,)),
            dma((2, big)),
            dma((2, big)),
            dma((2, big)),
            dma((2, big)),
            dma((2, 2, big)),
            dma((2, 2, big)),
            dma((heads,)),
            dma((heads, nx, 2)),
            dma((heads, ntp)),
            dma((ntp, heads)),
        ],
        compiler_params=pltpu.CompilerParams(
            collective_id=0 if packed == FEW else 1,
            has_side_effects=True,
            vmem_limit_bytes=60 * 2**20,
        ),
    )(*lists, *tables, queries, keys, values)


FEW = 3
FEW_ROW = 5
FEW_SLOTS = 20


def plan(nz, ny, heads, blocks_dev, vert, counts, vert_v, counts_v, pack, row_pack, slot_at, starts, few, wide, wide_n, listed):
    all_heads = vert.shape[1]
    seq, tp = lax.axis_index("seq"), lax.axis_index("tp")
    quad = NV // 2
    wide[...] = jnp.zeros_like(wide)
    wide_n[...] = jnp.ones_like(wide_n)
    wide[:, :all_heads] = vert_v[...]
    wide_n[:, :all_heads] = jnp.broadcast_to(counts_v[0:1, :], (NV, all_heads))
    used = wide_n[...]
    slot = lax.broadcasted_iota(jnp.int32, used.shape, 0)
    lane = lax.broadcasted_iota(jnp.int32, used.shape, 1)
    h = lane % heads

    def whole(a, by):
        return ((a.astype(jnp.float32) + 0.5) * (1.0 / by)).astype(jnp.int32)

    device = whole(wide[...], blocks_dev)
    at_z = whole(device, ny)
    wanted = (slot < used) & ((slot > 0) | (h == 0))
    before = jnp.zeros_like(used)
    for dh in range(1, heads):
        before = before + jnp.where(h >= dh, pltpu.roll(used - 1, dh, 1), 0)
    position = jnp.where(slot == 0, 0, before + slot)
    few_half = FEW_SLOTS // 2
    late = position - NV
    upper = jnp.where(late < 0, position - quad, late - (few_half - quad)) >= 0
    alone = -1 - slot - NV * h
    owner = jnp.where(wanted, device, alone)
    row = jnp.where(wanted, jnp.where(upper, nz + device - at_z * ny, at_z), alone)
    rank = jnp.zeros_like(owner)
    row_rank = jnp.zeros_like(owner)
    for dh in range(heads):
        moved = pltpu.roll(owner, dh, 1) if dh else owner
        moved_row = pltpu.roll(row, dh, 1) if dh else row
        for dj in range(1 - NV, NV if dh else 0):
            here = (h >= dh) & (slot + dj >= 0) & (slot + dj < NV)
            by = (NV - dj) % NV
            other = pltpu.roll(moved, by, 0) if by else moved
            other_row = pltpu.roll(moved_row, by, 0) if by else moved_row
            rank = rank + (here & (other == owner)).astype(jnp.int32)
            row_rank = row_rank + (here & (other_row == row)).astype(jnp.int32)
    over = (rank >= FEW) | (row_rank >= FEW_ROW) | (before + used > FEW_SLOTS)
    is_few = jnp.max(jnp.where((lane < all_heads) & over, 1, 0)) == 0
    few[0] = is_few.astype(jnp.int32)

    @pl.loop(0, heads * NV)
    def _(p):
        listed[p] = 0

    end = jnp.int32(1)
    for head in range(heads):
        starts[head] = end
        n = counts[0, tp * heads + head]
        for j in range(1, NV):

            @pl.when(j < n)
            def _(j=j, head=head, end=end):
                listed[end + j - 1] = vert[j, tp * heads + head]

        end = end + n - 1

    def split(block):
        by = lax.div(block, blocks_dev)
        z = lax.div(by, ny)
        return by, z, by - z * ny

    def tables(slots, packed, row_packed):
        half = slots // 2
        sparse = packed == FEW
        for side in (0, 1):

            def at(i, side=side):
                return jnp.where(i < quad, side * quad + i, NV + side * (half - quad) + i - quad)

            for k in range(packed):
                pack[side, k] = 0
            for k in range(row_packed):
                row_pack[side, k] = 0

            @pl.loop(0, half)
            def _(i, side=side, at=at):
                p = at(i)
                owner, z, y = split(listed[p])
                first, second = (y, z) if side == 0 else (z, y)
                inside = listed[p] - owner * blocks_dev
                my_second = lax.div(seq, ny) if side == 0 else lax.rem(seq, ny)
                real = p < end

                def count(o, c):
                    other, oz, oy = split(listed[at(o)])
                    same = (other == owner) & real
                    same_row = ((oz if side == 0 else oy) == second) & real
                    return c[0] + same.astype(jnp.int32), c[1] + same_row.astype(jnp.int32)

                if sparse:
                    place, row_place = lax.fori_loop(0, i, count, (jnp.int32(0), jnp.int32(0)))
                else:
                    place = row_place = i

                @pl.when((owner == seq) & real)
                def _():
                    pack[side, place] = inside

                @pl.when((second == my_second) & real)
                def _():
                    row_pack[side, row_place] = first * packed + place

                slot_at[side, i] = second * row_packed + row_place

    @pl.when(is_few)
    def _():
        tables(FEW_SLOTS, FEW, FEW_ROW)

    @pl.when(jnp.logical_not(is_few))
    def _():
        tables(heads * NV, heads * NV // 2, heads * NV // 2)


def per_device(nz, ny, ntp, queries, keys, values, vertical, slash, counts):
    tok, width = queries.shape
    heads = width // HD
    half = heads * NV // 2
    lists = (vertical.T, slash.T, counts.T)
    table = jax.ShapeDtypeStruct((2, half), jnp.int32)
    smem = pl.BlockSpec(memory_space=pltpu.SMEM)
    vmem = pl.BlockSpec(memory_space=pltpu.VMEM)
    *tables, few = pl.pallas_call(
        functools.partial(plan, nz, ny, heads, tok // BLK),
        out_shape=(table,) * 3
        + (jax.ShapeDtypeStruct((heads,), jnp.int32), jax.ShapeDtypeStruct((1,), jnp.int32)),
        in_specs=[smem, smem, vmem, vmem],
        out_specs=(smem,) * 5,
        scratch_shapes=[
            pltpu.VMEM((NV, HD), jnp.int32),
            pltpu.VMEM((NV, HD), jnp.int32),
            pltpu.SMEM((heads * NV,), jnp.int32),
        ],
    )(lists[0], lists[2], lists[0], lists[2])

    def sparse(tables, *args):
        return attend(nz, ny, ntp, FEW_SLOTS, FEW, FEW_ROW, lists, tables, *args)

    def dense(tables, *args):
        return attend(nz, ny, ntp, heads * NV, half, half, lists, tables, *args)

    return lax.cond(few[0] > 0, sparse, dense, tables, queries, keys, values)


def solution(mesh):
    nseq, ntp = mesh.shape["seq"], mesh.shape["tp"]
    ny = 1 << ((nseq.bit_length() - 1 + 1) // 2)
    return jax.shard_map(
        functools.partial(per_device, nseq // ny, ny, ntp),
        mesh=mesh,
        in_specs=(P("seq", "tp"), P("seq", "tp"), P("seq", "tp"), P(), P(), P()),
        out_specs=P(("seq", "tp"), None),
        check_vma=False,
    )
```

```python
import functools
import math

import jax
import jax.numpy as jnp
from jax import lax
from jax.experimental import pallas as pl
from jax.experimental.pallas import tpu as pltpu
from jax.sharding import PartitionSpec as P

HD = 128
BLK = 64
NV = 8
NS = 2
SREACH = 8
HALO = SREACH * BLK

BIG = 1 << 30
NEG = -1e30
PACK, ROW_PACK, SLOT_AT, START, USED, LISTS, TABLE_ROWS = 0, 2, 4, 6, 7, 8, 12
EXP2_SCALE = math.log2(math.e) / math.sqrt(HD)
MESH = pl.DeviceIdType.MESH


def attend_tile(row0, tile, head, slot0, refs):
    q_ref, wk, wv, kv, kpos_v, kpos_s, off_ref, seq0 = refs
    q = q_ref[pl.ds(row0, tile), pl.ds(pl.multiple_of(head * HD, HD), HD)]
    rows = lax.broadcasted_iota(jnp.int32, (tile, HD), 0) + (seq0 + row0)
    kt = (((1,), (1,)), ((), ()))
    rest = (NV - 1) * BLK
    vert_k = jnp.concatenate([kv[0, :BLK], kv[pl.ds(slot0, NV - 1), :BLK].reshape(rest, HD)], axis=0)
    vert_v = jnp.concatenate([kv[0, BLK:], kv[pl.ds(slot0, NV - 1), BLK:].reshape(rest, HD)], axis=0)
    sv = lax.dot_general(q, vert_k, kt, preferred_element_type=jnp.float32)
    pair = 2 * BLK
    r_i = lax.broadcasted_iota(jnp.int32, (pair, HD), 0)
    c_i = lax.broadcasted_iota(jnp.int32, (pair, HD), 1)
    straight = (r_i < BLK) == (c_i < BLK)
    off0, off1 = off_ref
    vals = []
    ss = []
    for p in range(tile // pair):
        start = row0 + p * pair + HALO
        s0 = start + off0 * -BLK
        s1 = start + off1 * -BLK
        s1b = s1 + BLK
        k2 = jnp.concatenate(
            [wk[pl.ds(s0, pair), :], wk[pl.ds(s1b, BLK), :], wk[pl.ds(s1, BLK), :]], axis=0
        )
        v2 = jnp.concatenate(
            [wv[pl.ds(s0, pair), :], wv[pl.ds(s1b, BLK), :], wv[pl.ds(s1, BLK), :]], axis=0
        )
        both = lax.dot_general(
            q[p * pair : (p + 1) * pair], k2, kt, preferred_element_type=jnp.float32
        )
        score = jnp.where(straight, both[:, :pair], both[:, pair:])
        block = (row0 + p * pair) // BLK
        kp0 = jnp.broadcast_to(kpos_s[pl.ds(block, 1), :], (BLK, HD))
        kp1 = jnp.broadcast_to(kpos_s[pl.ds(block + 1, 1), :], (BLK, HD))
        kp = jnp.concatenate([kp0, kp1], axis=0)
        ss.append(jnp.where(kp <= rows[p * pair : (p + 1) * pair], score, NEG))
        vals.append(v2)
    ss = jnp.concatenate(ss, axis=0)
    parts = []
    for k in range(NV * BLK // HD):
        kp = kpos_v[0:1, k * HD : (k + 1) * HD]
        parts.append(jnp.where(kp <= rows, sv[:, k * HD : (k + 1) * HD], NEG))
    top = ss
    for part in parts:
        top = jnp.maximum(top, part)
    top = jnp.max(top, axis=1, keepdims=True)
    ps = jnp.exp2((ss - top) * EXP2_SCALE)
    total = ps
    probs = []
    for part in parts:
        prob = jnp.exp2((part - top) * EXP2_SCALE)
        total = total + prob
        probs.append(prob.astype(jnp.bfloat16))
    total = jnp.sum(total, axis=1, keepdims=True)
    acc = jnp.dot(
        jnp.concatenate(probs, axis=1), vert_v, preferred_element_type=jnp.float32
    )
    slash_acc = []
    for p in range(tile // pair):
        w = ps[p * pair : (p + 1) * pair]
        w2 = jnp.concatenate(
            [
                jnp.where(straight, w, 0.0).astype(jnp.bfloat16),
                jnp.where(straight, 0.0, w).astype(jnp.bfloat16),
            ],
            axis=1,
        )
        slash_acc.append(jnp.dot(w2, vals[p], preferred_element_type=jnp.float32))
    acc = acc + jnp.concatenate(slash_acc, axis=0)
    return (acc / total).astype(jnp.bfloat16)


def key_positions(h, heads, seq, blocks_dev, table, kpos_v, kpos_s):
    n_vert = table[USED, h]
    n_slash = table[USED, heads + h]
    lane = lax.broadcasted_iota(jnp.int32, (8, HD), 1)
    for k in range(NV // 2):
        pos = jnp.where(lane < BLK, table[LISTS + h, 2 * k], table[LISTS + h, 2 * k + 1]) * BLK + lane % BLK
        used = jnp.where(lane < BLK, 2 * k, 2 * k + 1) < n_vert
        kpos_v[:, k * HD : (k + 1) * HD] = jnp.where(used, pos, BIG)
    row = lax.broadcasted_iota(jnp.int32, (blocks_dev, HD), 0)
    col = lax.broadcasted_iota(jnp.int32, (blocks_dev, HD), 1)
    first = (row % 2 == 0) == (col < BLK)
    block = seq * blocks_dev + row - jnp.where(first, table[USED, 2 * heads + h], table[USED, 3 * heads + h])
    dead = (block < 0) | (jnp.where(first, 0, 1) >= n_slash)
    for j in range(NV):
        dead = dead | ((block == table[LISTS + h, j]) & (jnp.full_like(row, j) < n_vert))
    kpos_s[...] = jnp.where(dead, BIG, block * BLK + col % BLK)


def fused(
    nz, ny, ntp, slots, packed, row_packed,
    table, q_hbm, k_hbm, v_hbm, out,
    q_ref, wk, wv, hk, hv, snd, got1k, got1v, mid, got2k, got2v, col, kv,
    obuf, obox, kpos_v, kpos_s,
    local_sem, halo_send, halo_recv, send1, recv1, send2, recv2, send3, recv3,
    own_sem, out_send, out_recv, place_sem,
):
    tok = q_ref.shape[0]
    heads = q_ref.shape[1] // HD
    blocks_dev = tok // BLK
    half = slots // 2
    quad = NV // 2
    seq = lax.axis_index("seq")
    tp = lax.axis_index("tp")
    z, y = seq // ny, lax.rem(seq, ny)
    nseq = nz * ny
    axes = ((ny, nz), (nz, ny))
    mine = ((y, z), (z, y))
    got1, got2 = (got1k, got1v), (got2k, got2v)

    def at(side, first, second):
        return (second * ny + first if side == 0 else first * ny + second, tp)

    def local(i, src, dst):
        return pltpu.make_async_copy(src, dst, local_sem.at[i])

    copies = [
        local(0, k_hbm, wk.at[HALO:]),
        local(1, v_hbm, wv.at[HALO:]),
        local(2, q_hbm, q_ref),
    ]
    for c in copies[:2]:
        c.start()

    def far_first(n):
        return sorted(range(1, n), key=lambda d: -min(d, n - d))

    barrier = pltpu.get_barrier_semaphore()
    for d in far_first(max(ny, nz)):
        for peer in ((z * ny + lax.rem(y + d, ny)), (lax.rem(z + d, nz) * ny + y)):
            pl.semaphore_signal(barrier, inc=1, device_id=(peer, tp), device_id_type=MESH)

    after, before = lax.rem(seq + 1, nseq), lax.rem(seq + nseq - 1, nseq)
    for peer in (after, before):
        pl.semaphore_signal(barrier, inc=1, device_id=(peer, tp), device_id_type=MESH)
    for d in far_first(ntp):
        pl.semaphore_signal(
            barrier, inc=1, device_id=(seq, lax.rem(tp + d, ntp)), device_id_type=MESH
        )
    copies[2].start()

    kv[slots:] = jnp.zeros_like(kv[slots:])
    copies[0].wait()
    copies[1].wait()

    for side in (0, 1):
        n = axes[side][0]
        piece = 2 * BLK // n

        @pl.loop(0, packed)
        def _(k, side=side, n=n, piece=piece):
            row = table[PACK + side, k] * BLK + HALO
            rows_k = wk[pl.ds(row, BLK), :]
            rows_v = wv[pl.ds(row, BLK), :]
            for c in range(n):
                rows, at_row = (rows_k, c * piece) if c < n // 2 else (rows_v, c * piece - BLK)
                snd[side, c, k] = rows[at_row : at_row + piece]

    pl.semaphore_wait(barrier, ny + nz + ntp - 3 + 2)

    halo = [
        pltpu.make_async_remote_copy(
            src_ref=w.at[tok : tok + HALO],
            dst_ref=dst,
            send_sem=halo_send.at[i],
            recv_sem=halo_recv.at[i],
            device_id=(after, tp),
            device_id_type=MESH,
        )
        for i, (w, dst) in enumerate(((wk, hk), (wv, hv)))
    ]

    def spread1(side, d):
        n, me = axes[side][0], mine[side][0]
        peer = lax.rem(me + d, n)
        return pltpu.make_async_remote_copy(
            src_ref=snd.at[side, peer],
            dst_ref=got1[side].at[pl.ds(me * packed, packed)],
            send_sem=send1.at[side, d],
            recv_sem=recv1.at[side, n - d],
            device_id=at(side, peer, mine[side][1]),
            device_id_type=MESH,
        )

    def gather2(side, d):
        n, me = axes[side][1], mine[side][1]
        peer = lax.rem(me + d, n)
        return pltpu.make_async_remote_copy(
            src_ref=mid.at[side],
            dst_ref=got2[side].at[pl.ds(me * row_packed, row_packed)],
            send_sem=send2.at[side, d],
            recv_sem=recv2.at[side, n - d],
            device_id=at(side, mine[side][0], peer),
            device_id_type=MESH,
        )

    def rows_of(side):
        n, me = axes[side][0], mine[side][0]
        piece = 2 * BLK // n
        return pl.ds(pl.multiple_of(me * piece, 16), piece)

    more = half - quad

    def parts(chunk, side):
        if chunk == 0:
            return pl.ds(0, quad), pl.ds(side * quad, quad)
        return pl.ds(quad, more), pl.ds(NV + side * more, more)

    def gather1(chunk, side, d):
        n, me = axes[side][0], mine[side][0]
        src, dst = parts(chunk, side)
        return pltpu.make_async_remote_copy(
            src_ref=col.at[side, src],
            dst_ref=kv.at[dst, rows_of(side)],
            send_sem=send3.at[chunk, side, d],
            recv_sem=recv3.at[chunk, side, n - d],
            device_id=at(side, lax.rem(me + d, n), mine[side][1]),
            device_id_type=MESH,
        )

    def each(axis, step):
        for d in far_first(max(ny, nz)):
            for side in (0, 1):
                if d < axes[side][axis]:
                    step(side, d)

    each(0, lambda side, d: spread1(side, d).start())
    halo[0].start()

    for side in (0, 1):
        me = mine[side][0]
        got1[side][pl.ds(me * packed, packed)] = snd[side, me]
    for side in (0, 1):
        for d in range(1, axes[side][0]):
            spread1(side, d).wait_recv()
        for k in range(row_packed):
            mid[side, k] = got1[side][table[ROW_PACK + side, k]]
        for d in far_first(axes[side][1]):
            gather2(side, d).start()
    halo[1].start()

    for side in (0, 1):
        me = mine[side][1]
        got2[side][pl.ds(me * row_packed, row_packed)] = mid[side]
    for side in (0, 1):
        for d in range(1, axes[side][1]):
            gather2(side, d).wait_recv()
        for i in range(half):
            col[side, i] = got2[side][table[SLOT_AT + side, i]]
        for d in far_first(axes[side][0]):
            gather1(0, side, d).start()
    each(0, lambda side, d: gather1(1, side, d).start())
    for chunk in (0, 1):
        for side in (0, 1):
            src, dst = parts(chunk, side)
            kv[dst, rows_of(side)] = col[side, src]

    for c in halo:
        c.wait_recv()
    joins = [local(3, hk, wk.at[0:HALO]), local(4, hv, wv.at[0:HALO])]
    for c in joins:
        c.start()
    copies[2].wait()
    for c in joins:
        c.wait()

    nx = ntp // 2
    part = tok // ntp
    tile = 2 * part
    x, core = tp // 2, lax.rem(tp, 2)
    order = (2, 1, 3, 0) if nx == 4 else tuple(range(nx - 1, -1, -1))

    def send_out(h, j, c, target):
        src = pl.multiple_of(c * part, 16)
        return pltpu.make_async_remote_copy(
            src_ref=obuf.at[h, j, pl.ds(src, part), :],
            dst_ref=obox.at[tp, h],
            send_sem=out_send.at[h, j, c],
            recv_sem=out_recv.at[h, tp],
            device_id=(seq, target),
            device_id_type=MESH,
        )

    def keep_out(h, j):
        src = pl.multiple_of(core * part, 16)
        cols = pl.ds(pl.multiple_of((tp * heads + h) * HD, HD), HD)
        return pltpu.make_async_copy(
            obuf.at[h, j, pl.ds(src, part), :], out.at[:, cols], own_sem.at[h]
        )

    def place_out(h, source):
        cols = pl.ds(pl.multiple_of((source * heads + h) * HD, HD), HD)
        return pltpu.make_async_copy(obox.at[source, h], out.at[:, cols], place_sem.at[source, h])

    def landed(h, source):
        return pltpu.make_async_remote_copy(
            src_ref=obuf.at[h, 0, pl.ds(0, part), :],
            dst_ref=obox.at[source, h],
            send_sem=out_send.at[h, 0, 0],
            recv_sem=out_recv.at[h, source],
            device_id=(seq, source),
            device_id_type=MESH,
        )

    def run_head(h, slot0):
        key_positions(h, heads, seq, blocks_dev, table, kpos_v, kpos_s)
        if isinstance(h, int):
            each(0, lambda side, d: gather1(0, side, d).wait_recv())
        refs = (
            q_ref, wk, wv, kv, kpos_v, kpos_s,
            (table[USED, 2 * heads + h], table[USED, 3 * heads + h]), seq * tok,
        )
        for j, step in enumerate(order):
            chip = lax.rem(x + step, nx)
            row0 = pl.multiple_of(chip * tile, BLK)
            obuf[h, j] = attend_tile(row0, tile, h, slot0, refs)
            if step:
                for c in (0, 1):
                    send_out(h, j, c, chip * 2 + c).start()
            else:
                send_out(h, j, 1 - core, chip * 2 + 1 - core).start()
                keep_out(h, j).start()

    run_head(0, 1)
    each(0, lambda side, d: gather1(1, side, d).wait_recv())

    @pl.loop(1, heads)
    def _(h):
        run_head(h, table[START, h])

    @pl.loop(0, heads)
    def _(h):
        @pl.loop(1, ntp)
        def _(d):
            source = lax.rem(tp + d, ntp)
            landed(h, source).wait_recv()
            place_out(h, source).start()

    @pl.loop(0, heads)
    def _(h):
        @pl.loop(1, ntp)
        def _(d):
            place_out(h, lax.rem(tp + d, ntp)).wait()

        keep_out(h, nx - 1).wait()
        for j, step in enumerate(order):
            chip = lax.rem(x + step, nx)
            if step:
                for c in (0, 1):
                    send_out(h, j, c, chip * 2 + c).wait_send()
            else:
                send_out(h, j, 1 - core, chip * 2 + 1 - core).wait_send()

    for c in halo:
        c.wait_send()
    each(0, lambda side, d: spread1(side, d).wait_send())
    each(1, lambda side, d: gather2(side, d).wait_send())
    for chunk in (0, 1):
        each(0, lambda side, d: gather1(chunk, side, d).wait_send())


def attend(nz, ny, ntp, slots, packed, row_packed, table, queries, keys, values):
    tok, width = queries.shape
    heads = width // HD
    part = tok // ntp
    nx = ntp // 2
    big = max(ny, nz)
    half = slots // 2
    pieces = [2 * BLK // n for n in (ny, nz)]
    dma = pltpu.SemaphoreType.DMA
    bf = jnp.bfloat16
    smem = pl.BlockSpec(memory_space=pltpu.SMEM)
    hbm = pl.BlockSpec(memory_space=pltpu.HBM)
    return pl.pallas_call(
        functools.partial(fused, nz, ny, ntp, slots, packed, row_packed),
        out_shape=jax.ShapeDtypeStruct((part, width * ntp), bf),
        in_specs=[smem] + [hbm] * 3,
        out_specs=pl.BlockSpec(memory_space=pl.ANY),
        scratch_shapes=[
            pltpu.VMEM((tok, width), bf),
            pltpu.VMEM((HALO + tok, HD), bf),
            pltpu.VMEM((HALO + tok, HD), bf),
            pltpu.VMEM((HALO, HD), bf),
            pltpu.VMEM((HALO, HD), bf),
            pltpu.VMEM((2, big, packed, pieces[0], HD), bf),
            pltpu.VMEM((ny * packed, pieces[0], HD), bf),
            pltpu.VMEM((nz * packed, pieces[1], HD), bf),
            pltpu.VMEM((2, row_packed, pieces[0], HD), bf),
            pltpu.VMEM((nz * row_packed, pieces[0], HD), bf),
            pltpu.VMEM((ny * row_packed, pieces[1], HD), bf),
            pltpu.VMEM((2, half, pieces[0], HD), bf),
            pltpu.VMEM((slots + NV, 2 * BLK, HD), bf),
            pltpu.VMEM((heads, nx, 2 * part, HD), bf),
            pltpu.VMEM((ntp, heads, part, HD), bf),
            pltpu.VMEM((8, NV * BLK), jnp.int32),
            pltpu.VMEM((tok // BLK, HD), jnp.int32),
            dma((5,)),
            dma((2,)),
            dma((2,)),
            dma((2, big)),
            dma((2, big)),
            dma((2, big)),
            dma((2, big)),
            dma((2, 2, big)),
            dma((2, 2, big)),
            dma((heads,)),
            dma((heads, nx, 2)),
            dma((heads, ntp)),
            dma((ntp, heads)),
        ],
        compiler_params=pltpu.CompilerParams(
            collective_id=0 if packed == FEW else 1,
            has_side_effects=True,
            vmem_limit_bytes=60 * 2**20,
        ),
    )(table, queries, keys, values)


FEW = 3
FEW_ROW = 5
FEW_SLOTS = 20


def plan(nz, ny, heads, blocks_dev, vert, slash, counts, vert_v, counts_v, table, few, wide, wide_n, listed):
    all_heads = vert.shape[1]
    seq, tp = lax.axis_index("seq"), lax.axis_index("tp")
    quad = NV // 2
    wide[...] = jnp.zeros_like(wide)
    wide_n[...] = jnp.ones_like(wide_n)
    wide[:, :all_heads] = vert_v[...]
    wide_n[:, :all_heads] = jnp.broadcast_to(counts_v[0:1, :], (NV, all_heads))
    used = wide_n[...]
    slot = lax.broadcasted_iota(jnp.int32, used.shape, 0)
    lane = lax.broadcasted_iota(jnp.int32, used.shape, 1)
    h = lane % heads

    def whole(a, by):
        return ((a.astype(jnp.float32) + 0.5) * (1.0 / by)).astype(jnp.int32)

    device = whole(wide[...], blocks_dev)
    at_z = whole(device, ny)
    wanted = (slot < used) & ((slot > 0) | (h == 0))
    before = jnp.zeros_like(used)
    for dh in range(1, heads):
        before = before + jnp.where(h >= dh, pltpu.roll(used - 1, dh, 1), 0)
    position = jnp.where(slot == 0, 0, before + slot)
    few_half = FEW_SLOTS // 2
    late = position - NV
    upper = jnp.where(late < 0, position - quad, late - (few_half - quad)) >= 0
    alone = -1 - slot - NV * h
    owner = jnp.where(wanted, device, alone)
    row = jnp.where(wanted, jnp.where(upper, nz + device - at_z * ny, at_z), alone)
    rank = jnp.zeros_like(owner)
    row_rank = jnp.zeros_like(owner)
    for dh in range(heads):
        moved = pltpu.roll(owner, dh, 1) if dh else owner
        moved_row = pltpu.roll(row, dh, 1) if dh else row
        for dj in range(1 - NV, NV if dh else 0):
            here = (h >= dh) & (slot + dj >= 0) & (slot + dj < NV)
            by = (NV - dj) % NV
            other = pltpu.roll(moved, by, 0) if by else moved
            other_row = pltpu.roll(moved_row, by, 0) if by else moved_row
            rank = rank + (here & (other == owner)).astype(jnp.int32)
            row_rank = row_rank + (here & (other_row == row)).astype(jnp.int32)
    over = (rank >= FEW) | (row_rank >= FEW_ROW) | (before + used > FEW_SLOTS)
    is_few = jnp.max(jnp.where((lane < all_heads) & over, 1, 0)) == 0
    few[0] = is_few.astype(jnp.int32)

    for p in range(heads * NV):
        listed[p] = 0
    end = jnp.int32(1)
    for head in range(heads):
        at = tp * heads + head
        n = counts[0, at]
        table[START, head] = end
        table[USED, head] = n
        table[USED, heads + head] = counts[1, at]
        for j in range(NS):
            table[USED, (2 + j) * heads + head] = slash[j, at]
        table[LISTS + head, 0] = vert[0, at]
        for j in range(1, NV):
            block = vert[j, at]
            table[LISTS + head, j] = block

            @pl.when(j < n)
            def _(j=j, end=end, block=block):
                listed[end + j - 1] = block

        end = end + n - 1
    my_z = lax.div(seq, ny)
    my_y = seq - my_z * ny

    def split(block):
        by = lax.div(block, blocks_dev)
        z = lax.div(by, ny)
        return by, z, by - z * ny

    def place_at(side, half, i):
        return side * quad + i if i < quad else NV + side * (half - quad) + i - quad

    def tables(slots, packed, row_packed):
        half = slots // 2
        sparse = packed == FEW
        for side in (0, 1):
            mine = my_z if side == 0 else my_y
            if sparse:
                for k in range(packed):
                    table[PACK + side, k] = 0
                for k in range(row_packed):
                    table[ROW_PACK + side, k] = 0
            owners, rows = [], []
            for i in range(half):
                p = place_at(side, half, i)
                block = listed[p]
                owner, z, y = split(block)
                first, second = (y, z) if side == 0 else (z, y)
                inside = block - owner * blocks_dev
                if not sparse:
                    table[PACK + side, i] = inside
                    table[ROW_PACK + side, i] = first * packed + i
                    table[SLOT_AT + side, i] = second * row_packed + i
                    continue
                real = (p < end).astype(jnp.int32)
                place = row_place = jnp.int32(0)
                for other, other_row in zip(owners, rows):
                    place = place + (other == owner).astype(jnp.int32)
                    row_place = row_place + (other_row == second).astype(jnp.int32)
                owners.append(owner)
                rows.append(second)
                place, row_place = place * real, row_place * real
                table[SLOT_AT + side, i] = second * row_packed + row_place

                @pl.when((owner == seq) & (p < end))
                def _(place=place, inside=inside, side=side):
                    table[PACK + side, place] = inside

                @pl.when((second == mine) & (p < end))
                def _(place=place, row_place=row_place, first=first, side=side):
                    table[ROW_PACK + side, row_place] = first * packed + place

    @pl.when(is_few)
    def _():
        tables(FEW_SLOTS, FEW, FEW_ROW)

    @pl.when(jnp.logical_not(is_few))
    def _():
        tables(heads * NV, heads * NV // 2, heads * NV // 2)


def per_device(nz, ny, ntp, queries, keys, values, vertical, slash, counts):
    tok, width = queries.shape
    heads = width // HD
    half = heads * NV // 2
    lists = (vertical.T, slash.T, counts.T)
    smem = pl.BlockSpec(memory_space=pltpu.SMEM)
    vmem = pl.BlockSpec(memory_space=pltpu.VMEM)
    table, few = pl.pallas_call(
        functools.partial(plan, nz, ny, heads, tok // BLK),
        out_shape=(
            jax.ShapeDtypeStruct((TABLE_ROWS, half), jnp.int32),
            jax.ShapeDtypeStruct((1,), jnp.int32),
        ),
        in_specs=[smem, smem, smem, vmem, vmem],
        out_specs=(smem, smem),
        scratch_shapes=[
            pltpu.VMEM((NV, HD), jnp.int32),
            pltpu.VMEM((NV, HD), jnp.int32),
            pltpu.SMEM((heads * NV,), jnp.int32),
        ],
    )(*lists, lists[0], lists[2])

    def sparse(*args):
        return attend(nz, ny, ntp, FEW_SLOTS, FEW, FEW_ROW, *args)

    def dense(*args):
        return attend(nz, ny, ntp, heads * NV, half, half, *args)

    return lax.cond(few[0] > 0, sparse, dense, table, queries, keys, values)


def solution(mesh):
    nseq, ntp = mesh.shape["seq"], mesh.shape["tp"]
    ny = 1 << ((nseq.bit_length() - 1 + 1) // 2)
    return jax.shard_map(
        functools.partial(per_device, nseq // ny, ny, ntp),
        mesh=mesh,
        in_specs=(P("seq", "tp"), P("seq", "tp"), P("seq", "tp"), P(), P(), P()),
        out_specs=P(("seq", "tp"), None),
        check_vma=False,
    )
```
